512 devices in a mesh: row: 32 (over z_hi, x, core), col: 16 (over z_lo, y).
Axes of the slice: x: 4, y: 4, z: 16 (z_hi: 4, z_lo: 4; z = z_hi * 4 + z_lo), core: 2. Of those that a mesh axis runs over, the one named last changes fastest.
Arguments:
- features: bfloat16 [65536, 256], P(('col', 'row')), may hold values from -6 to 6
- weight: bfloat16 [256, 256], replicated, may hold values from -0.375 to 0.375
- grad_out: bfloat16 [65536, 256], P(('row', 'col')), may hold values from -6 to 6
- tiles: bfloat16 [32, 16, 128, 128, 128], P('row', 'col'), may hold values from -0.046875 to 0.046875
- tile_rows: int32 [32, 16, 128], P('row', 'col'), may hold values from 0 to 15, as said below
- tile_cols: int32 [32, 16, 128], P('row', 'col'), may hold values from 0 to 31, as said below
- tile_count: int32 [32, 16], P('row', 'col'), may hold values from 32 to 128, as said below
Outputs:
- hidden: bfloat16 [65536, 256], P(('row', 'col'))
- grad_features: bfloat16 [65536, 256], P(('col', 'row'))
- grad_weight: float32 [256, 256], replicated
The draws below stay inside these ranges and needn't reach their ends.
Inputs may be any that keep to these rules, and one draw needn't show every extreme that they name: `tile_rows`: within one block the live and unused slots all name distinct tile places. `tile_cols`: paired with tile_rows slot by slot. `tile_count`: some block is full in every draw.
All inputs are finite; a program needn't handle non-finite values.
Results may differ from the reference program's by a relative error of at most 0.03.
Values may be sent and summed in bfloat16 or wider, within the bound.
A program may use at most 64 MiB of HBM per device.

```python
import jax
import jax.numpy as jnp
from jax import lax

F = 256
TILE = 128
RT_BLK = 16
TILES_DEV = 128
COL_TILES = 32
NODES = 65536
N_ROW = 32
N_COL = 16


def placements(key):
    keys = jax.random.split(key, N_ROW * N_COL)
    orders = jax.vmap(lambda single: jax.random.permutation(single, RT_BLK * COL_TILES))(keys)
    return orders[:, :TILES_DEV].reshape(N_ROW, N_COL, TILES_DEV).astype(jnp.int32)


def draw_tile_rows(key, part):
    places = placements(key)
    return (places // COL_TILES).astype(jnp.int32)


def draw_tile_cols(key, part):
    places = placements(key)
    return (places % COL_TILES).astype(jnp.int32)


def draw_tile_count(key, part):
    key = jax.random.fold_in(key, 7)
    first, second = jax.random.split(key)
    counts = jax.random.randint(first, (N_ROW * N_COL,), TILES_DEV // 4, TILES_DEV + 1, dtype=jnp.int32)
    chosen = jax.random.randint(second, (), 0, N_ROW * N_COL, dtype=jnp.int32)
    places = jnp.arange(N_ROW * N_COL, dtype=jnp.int32)
    counts = jnp.where(places == chosen, TILES_DEV, counts)
    return counts.reshape(N_ROW, N_COL).astype(jnp.int32)


def level_of(rng, dims, pieces, low, high):
    loudness, own = 1.0, jax.random.fold_in(rng, 6)
    for position, shards_of in pieces:
        steps = jnp.exp(jax.random.uniform(jax.random.fold_in(own, position), (shards_of,), jnp.float32, low / len(pieces), high / len(pieces)))
        loudness = loudness * jnp.repeat(steps, dims[position] // shards_of).reshape([-1 if axis == position else 1 for axis in range(len(dims))])
    return loudness


def scatter_about(rng, extent, deviation, limit, pieces=(), kind=jnp.bfloat16):
    values = deviation * jax.random.normal(rng, extent, jnp.float32)
    if pieces:
        values = values * level_of(rng, extent, pieces, -0.22, 0.18)
    return jnp.clip(values, -limit, limit).astype(kind)


def setup_inputs(seed: int = 0) -> dict:
    key_list = jax.random.split(jax.random.key(seed), 8)
    features = scatter_about(key_list[0], (NODES, F), 1.0, 6.0, ((0, 512),))
    weight = scatter_about(key_list[1], (F, F), F ** -0.5, 0.375)
    grad_out = scatter_about(key_list[2], (NODES, F), 1.0, 6.0, ((0, 512),))
    tiles = scatter_about(key_list[3], (N_ROW, N_COL, TILES_DEV, TILE, TILE), (TILE * TILES_DEV * N_COL // RT_BLK) ** -0.5, 0.046875, ((0, 32), (1, 16)))
    tile_rows = draw_tile_rows(jax.random.fold_in(key_list[7], 71), 0)
    tile_cols = draw_tile_cols(jax.random.fold_in(key_list[7], 71), 0)
    tile_count = draw_tile_count(jax.random.fold_in(key_list[7], 71), 0)
    return {"features": features, "weight": weight, "grad_out": grad_out, "tiles": tiles, "tile_rows": tile_rows, "tile_cols": tile_cols, "tile_count": tile_count}


root_half = 0.7071067811865476
inv_root_tau = 0.3989422804014327

def activate(preact):
    return 0.5 * preact * (1.0 + lax.erf(preact * root_half))

def activate_grad(preact):
    return 0.5 * (1.0 + lax.erf(preact * root_half)) + preact * jnp.exp(-0.5 * preact * preact) * inv_root_tau

def spread(tiles_here, out_index, in_index, live_count, source, targets, flip):
    is_live = jnp.arange(tiles_here.shape[0], dtype=jnp.int32) < live_count
    picked = source[in_index].astype(jnp.float32)
    form = 'tji,tjf->tif' if flip else 'tij,tjf->tif'
    prods = jnp.einsum(form, tiles_here.astype(jnp.float32), picked, precision=lax.Precision.HIGHEST)
    select = ((out_index[None, :] == jnp.arange(targets, dtype=jnp.int32)[:, None]) & is_live[None, :]).astype(jnp.float32)
    totals = jnp.einsum('st,tif->sif', select, prods, precision=lax.Precision.HIGHEST)
    return totals.reshape(targets * prods.shape[1], prods.shape[2])

def reference(features, weight, grad_out, tiles, tile_rows, tile_cols, tile_count):
    x_blocks = features.reshape(N_COL, COL_TILES, TILE, F)

    def row_block(row_index):

        def col_part(col_index):
            part = spread(tiles[row_index, col_index], tile_rows[row_index, col_index], tile_cols[row_index, col_index], tile_count[row_index, col_index], x_blocks[col_index], RT_BLK, False)
            return part.astype(jnp.bfloat16)
        parts = lax.map(col_part, jnp.arange(N_COL, dtype=jnp.int32))
        return lax.optimization_barrier(jnp.sum(parts.astype(jnp.float32), axis=0)).astype(jnp.bfloat16)
    aggregate = lax.map(row_block, jnp.arange(N_ROW, dtype=jnp.int32)).reshape(NODES, F)
    preact = jnp.dot(aggregate, weight, preferred_element_type=jnp.float32)
    hidden = activate(preact).astype(jnp.bfloat16)
    pre_grad = (grad_out.astype(jnp.float32) * activate_grad(preact)).astype(jnp.bfloat16)
    grad_weight = lax.dot_general(aggregate, pre_grad, (((0,), (0,)), ((), ())), preferred_element_type=jnp.float32)
    prop_grad = lax.dot_general(pre_grad, weight, (((1,), (1,)), ((), ())), preferred_element_type=jnp.float32).astype(jnp.bfloat16)
    grad_blocks = prop_grad.reshape(N_ROW, RT_BLK, TILE, F)

    def col_block(col_index):

        def row_part(row_index):
            part = spread(tiles[row_index, col_index], tile_cols[row_index, col_index], tile_rows[row_index, col_index], tile_count[row_index, col_index], grad_blocks[row_index], COL_TILES, True)
            return part.astype(jnp.bfloat16)
        parts = lax.map(row_part, jnp.arange(N_ROW, dtype=jnp.int32))
        return lax.optimization_barrier(jnp.sum(parts.astype(jnp.float32), axis=0)).astype(jnp.bfloat16)
    grad_features = lax.map(col_block, jnp.arange(N_COL, dtype=jnp.int32)).reshape(NODES, F)
    return (hidden, grad_features, grad_weight)
```

```python
import functools

import jax
import jax.numpy as jnp
from jax import lax
from jax.experimental import pallas as pl
from jax.experimental.pallas import tpu as pltpu
from jax.sharding import PartitionSpec as P

MESH = pl.DeviceIdType.MESH
BF = jnp.bfloat16
F32 = jnp.float32
root_half = 0.7071067811865476
inv_root_tau = 0.3989422804014327
T = 128
H = 64
F = 256


class Place:
    def __init__(self):
        row, col = lax.axis_index("row"), lax.axis_index("col")
        self.zh, self.x, self.core = row // 8, (row // 2) % 4, row % 2
        self.zl, self.y = col // 4, col % 4

    def at(self, zh=None, x=None, core=None, zl=None, y=None):
        zh = self.zh if zh is None else zh % 4
        x = self.x if x is None else x % 4
        core = self.core if core is None else core
        zl = self.zl if zl is None else zl % 4
        y = self.y if y is None else y % 4
        return ((zh * 4 + x) * 2 + core, zl * 4 + y)


class Net:
    def __init__(self, send, recv):
        self.send, self.recv, self.started = send, recv, []

    def copy(self, src, dst, device):
        n = len(self.started)
        one = pltpu.make_async_remote_copy(
            src_ref=src,
            dst_ref=dst,
            send_sem=self.send.at[n],
            recv_sem=self.recv.at[n],
            device_id=device,
            device_id_type=MESH,
        )
        one.start()
        self.started.append(one)
        return one

    def drain(self):
        for one in self.started:
            one.wait_send()


def meet(partners):
    barrier = pltpu.get_barrier_semaphore()
    for device in partners:
        pl.semaphore_signal(barrier, inc=1, device_id=device, device_id_type=MESH)
    pl.semaphore_wait(barrier, len(partners))


class RingGather:
    def __init__(self, net, slot, p, dev):
        self.net, self.slot, self.p, self.dev = net, slot, p, dev

    def start(self):
        p, slot = self.p, self.slot
        self.up = self.net.copy(slot(p), slot(p), self.dev(p + 1))
        self.down = self.net.copy(slot(p), slot(p), self.dev(p - 1))

    def low(self):
        self.up.wait_recv()
        part = self.slot(self.p - 1).at[pl.ds(0, H)]
        self.up2 = self.net.copy(part, part, self.dev(self.p + 1))

    def high(self):
        self.down.wait_recv()
        part = self.slot(self.p + 1).at[pl.ds(H, H)]
        self.down2 = self.net.copy(part, part, self.dev(self.p - 1))

    def far(self):
        self.up2.wait_recv()
        self.down2.wait_recv()


class RingReduce:
    def __init__(self, net, src, land, pass_in, pass_out, p, dev):
        self.net, self.src, self.land, self.p, self.dev = net, src, land, p, dev
        self.pass_in, self.pass_out = pass_in, pass_out

    def start_far(self):
        p, src, net = self.p, self.src, self.net
        self.a = net.copy(src(p + 2, 0), self.pass_in.at[0], self.dev(p + 1))
        self.b = net.copy(src(p + 2, 1), self.pass_in.at[1], self.dev(p - 1))

    def start_near(self):
        p, src, net = self.p, self.src, self.net
        self.c1 = net.copy(src(p + 1, 1), self.land.at[0, 1], self.dev(p + 1))
        self.d0 = net.copy(src(p - 1, 0), self.land.at[1, 0], self.dev(p - 1))

    def mid(self):
        p, src, net = self.p, self.src, self.net
        self.a.wait_recv()
        total = src(p + 1, 0)[...].astype(F32) + self.pass_in[0].astype(F32)
        self.pass_out[0] = total.astype(BF)
        self.c0 = net.copy(self.pass_out.at[0], self.land.at[0, 0], self.dev(p + 1))
        self.b.wait_recv()
        total = src(p - 1, 1)[...].astype(F32) + self.pass_in[1].astype(F32)
        self.pass_out[1] = total.astype(BF)
        self.d1 = net.copy(self.pass_out.at[1], self.land.at[1, 1], self.dev(p - 1))

    def total(self, half):
        (self.c0 if half == 0 else self.c1).wait_recv()
        (self.d0 if half == 0 else self.d1).wait_recv()
        return (
            self.src(self.p, half)[...].astype(F32)
            + self.land[0, half].astype(F32)
            + self.land[1, half].astype(F32)
        )


def half_of(ref, half):
    return ref.at[pl.ds(half * H, H)]


def gather_x_kernel(own_ref, x_ref, send, recv):
    me = Place()
    net = Net(send, recv)
    sib = me.at(core=1 - me.core)
    meet([me.at(zh=me.zh + 1), me.at(zh=me.zh - 1), me.at(x=me.x + 1), me.at(x=me.x - 1), sib])
    x_ref[me.zh, me.x, me.core] = own_ref[...]

    def slot(zh, x):
        return x_ref.at[zh % 4, x % 4, me.core]

    across = []

    def swap(zh, x):
        across.append(net.copy(slot(zh, x), slot(zh, x), sib))

    rz = RingGather(net, lambda p: slot(p, me.x), me.zh, lambda p: me.at(zh=p))

    def ring_x(zh):
        ring = RingGather(net, lambda p: slot(zh, p), me.x, lambda p: me.at(x=p))
        ring.start()
        swap(zh, me.x)
        return ring

    def finish_x(ring, zh):
        ring.low()
        ring.high()
        swap(zh, me.x - 1)
        swap(zh, me.x + 1)

    def finish_far(ring, zh):
        ring.far()
        swap(zh, me.x + 2)

    rz.start()
    r0 = ring_x(me.zh)
    finish_x(r0, me.zh)
    finish_far(r0, me.zh)
    rz.low()
    r1 = ring_x(me.zh - 1)
    rz.high()
    r2 = ring_x(me.zh + 1)
    finish_x(r1, me.zh - 1)
    finish_x(r2, me.zh + 1)
    finish_far(r1, me.zh - 1)
    finish_far(r2, me.zh + 1)
    rz.far()
    r3 = ring_x(me.zh + 2)
    finish_x(r3, me.zh + 2)
    finish_far(r3, me.zh + 2)
    for one in across:
        one.wait_recv()
    net.drain()


def forward_kernel(place_ref, tiles_ref, x_ref, part_ref, tilebuf, dense, sem):
    load = pltpu.make_async_copy(tiles_ref, tilebuf.at[pl.ds(0, 128)], sem)
    load.start()
    tilebuf[128] = jnp.zeros((T, T), BF)
    load.wait()

    def build(r, _):
        for c in range(32):
            rows = pl.ds(pl.multiple_of(r * T, T), T)
            dense[c // 8, rows, pl.ds((c % 8) * T, T)] = tilebuf[place_ref[r * 32 + c]]
        return 0

    lax.fori_loop(0, 16, build, 0)

    def block(m, _):
        rows = pl.ds(pl.multiple_of(m * 512, 512), 512)
        total = jnp.zeros((512, F), F32)
        for zh in range(4):
            total += jnp.dot(dense[zh, rows], x_ref[zh], preferred_element_type=F32)
        part_ref[rows] = total.astype(BF)
        return 0

    lax.fori_loop(0, 4, block, 0)


def backward_kernel(place_ref, tiles_ref, g_ref, part_ref, tilebuf, dense, sem):
    load = pltpu.make_async_copy(tiles_ref, tilebuf.at[pl.ds(0, 128)], sem)
    load.start()
    tilebuf[128] = jnp.zeros((T, T), BF)
    load.wait()

    def turn(s, _):
        tilebuf[s] = tilebuf[s].T
        return 0

    lax.fori_loop(0, 128, turn, 0)

    def build(c, _):
        for r in range(16):
            rows = pl.ds(pl.multiple_of(c * T, T), T)
            dense[r // 4, rows, pl.ds((r % 4) * T, T)] = tilebuf[place_ref[r * 32 + c]]
        return 0

    lax.fori_loop(0, 32, build, 0)

    def block(m, _):
        rows = pl.ds(pl.multiple_of(m * 512, 512), 512)
        total = jnp.zeros((512, F), F32)
        for zl in range(4):
            total += jnp.dot(dense[zl, rows], g_ref[zl], preferred_element_type=F32)
        part_ref[rows] = total.astype(BF)
        return 0

    lax.fori_loop(0, 8, block, 0)


def layer_kernel(
    part_ref, w_ref, go_ref, hid_ref, g_ref, dw_ref, land, pass_in, pass_out, zsum, zland, send, recv
):
    me = Place()
    net = Net(send, recv)
    meet(
        [me.at(y=me.y + 1), me.at(y=me.y - 1), me.at(zl=me.zl + 1), me.at(zl=me.zl + 2), me.at(zl=me.zl + 3)]
    )
    rings = []
    for d in (1, 2, 3, 0):
        q = (me.zl + d) % 4

        def src(p, half, q=q):
            return half_of(part_ref.at[q, p % 4], half)

        rings.append(
            RingReduce(
                net, src, land.at[d], pass_in.at[d], pass_out.at[d], me.y, lambda p: me.at(y=p)
            )
        )
    for ring in rings:
        ring.start_far()
        ring.start_near()
    over = []
    for i, d in enumerate((1, 2, 3, 0)):
        rings[i].mid()
        if i:
            e = i - 1
            for half in range(2):
                zsum[e, pl.ds(half * H, H)] = rings[e].total(half).astype(BF)
            over.append(net.copy(zsum.at[e], zland.at[e], me.at(zl=me.zl + e + 1)))
    own = jnp.concatenate([rings[3].total(0), rings[3].total(1)], axis=0)
    for one in over:
        one.wait_recv()
    agg = (own + zland[0].astype(F32) + zland[1].astype(F32) + zland[2].astype(F32)).astype(BF)

    w = w_ref[...]
    pre = jnp.dot(agg, w, preferred_element_type=F32)
    erf = lax.erf(pre * root_half)
    slope = 0.5 * (1.0 + erf) + pre * jnp.exp(-0.5 * pre * pre) * inv_root_tau
    pre_grad = (go_ref[...].astype(F32) * slope).astype(BF)
    prop = lax.dot_general(pre_grad, w, (((1,), (1,)), ((), ())), preferred_element_type=F32)
    g_ref[me.zl, me.y] = prop.astype(BF)

    def slot(zl, y):
        return g_ref.at[zl % 4, y % 4]

    across = [
        net.copy(slot(me.zl, me.y), slot(me.zl, me.y), me.at(zl=me.zl + d)) for d in (1, 2, 3)
    ]

    def ring_y(zl):
        ring = RingGather(net, lambda p: slot(zl, p), me.y, lambda p: me.at(y=p))
        ring.start()
        return ring

    gathers = [ring_y(me.zl)]
    hid_ref[...] = (0.5 * pre * (1.0 + erf)).astype(BF)
    dw_ref[...] = lax.dot_general(agg, pre_grad, (((0,), (0,)), ((), ())), preferred_element_type=F32)
    for i, d in enumerate((1, 2, 3)):
        gathers[i].low()
        gathers[i].high()
        across[i].wait_recv()
        gathers.append(ring_y(me.zl - d))
    gathers[3].low()
    gathers[3].high()
    for ring in gathers:
        ring.far()
    net.drain()


def scatter_kernel(
    part_ref, dw_ref, gx_ref, gw_ref,
    cland, csum, land, pass_in, pass_out, zsum, zl_land, z_in, z_out,
    w1, w1in, w2, w2in, w3, w3in, w4in, w5in, w6, w7, send, recv,
):
    me = Place()
    net = Net(send, recv)
    sib = me.at(core=1 - me.core)
    meet(
        [sib]
        + [me.at(zh=me.zh + d) for d in (1, 2, 3)]
        + [me.at(x=me.x + d) for d in (1, 2, 3)]
        + [me.at(y=me.y + d) for d in (1, 2, 3)]
        + [me.at(zl=me.zl + d) for d in (1, 2, 3)]
    )
    order = (2, 1, 3, 0)
    swaps = []
    for i, d in enumerate(order):
        q = (me.zh + d) % 4
        swaps.append(net.copy(part_ref.at[q, :, 1 - me.core], cland.at[i], sib))
    a1 = net.copy(dw_ref.at[pl.ds(pl.multiple_of((1 - me.core) * T, T), T)], w1in, sib)

    rings = []
    for i, d in enumerate(order):
        q = (me.zh + d) % 4

        def src(p, half, i=i):
            return half_of(csum.at[i, p % 4], half)

        rings.append(
            RingReduce(net, src, land.at[i], pass_in.at[i], pass_out.at[i], me.x, lambda p: me.at(x=p))
        )

    def add_swap(i, d):
        q = (me.zh + d) % 4
        swaps[i].wait_recv()
        csum[i] = (part_ref[q, :, me.core].astype(F32) + cland[i].astype(F32)).astype(BF)
        rings[i].start_far()
        rings[i].start_near()

    def zsrc(p, half):
        return half_of(zsum.at[p % 4], half)

    zring = RingReduce(net, zsrc, zl_land, z_in, z_out, me.zh, lambda p: me.at(zh=p))

    def total_x(i, d):
        for half in range(2):
            zsum[(me.zh + d) % 4, pl.ds(half * H, H)] = rings[i].total(half).astype(BF)

    def w_core():
        a1.wait_recv()
        w1[...] = dw_ref[pl.ds(pl.multiple_of(me.core * T, T), T)] + w1in[...]

    def piece(ref, p, n):
        return ref.at[pl.ds(pl.multiple_of((p % 4) * n, n), n)]

    def w_spread(src, land_ref, p, dev, n):
        return [net.copy(piece(src, p + d, n), land_ref.at[d - 1], dev(p + d)) for d in (1, 2, 3)]

    def w_join(copies, src, land_ref, p, n, dst):
        for one in copies:
            one.wait_recv()
        dst[...] = piece(src, p, n)[...] + land_ref[0] + land_ref[1] + land_ref[2]

    def w_all(slots, p, dev):
        mine = slots.at[p]
        return [net.copy(mine, mine, dev(p + d)) for d in (1, 2, 3)]

    def w_sum(copies, slots):
        for one in copies:
            one.wait_recv()
        return slots[0] + slots[1] + slots[2] + slots[3]

    dev_x = lambda p: me.at(x=p)
    dev_y = lambda p: me.at(y=p)
    dev_zl = lambda p: me.at(zl=p)
    dev_zh = lambda p: me.at(zh=p)

    add_swap(0, order[0])
    add_swap(1, order[1])
    w_core()
    a2 = w_spread(w1, w2in, me.x, dev_x, 32)
    add_swap(2, order[2])
    add_swap(3, order[3])
    rings[0].mid()
    rings[1].mid()
    w_join(a2, w1, w2in, me.x, 32, w2)
    a3 = w_spread(w2, w3in, me.y, dev_y, 8)
    total_x(0, order[0])
    zring.start_far()
    rings[2].mid()
    w_join(a3, w2, w3in, me.y, 8, w3)
    w4in[me.zl] = w3[...]
    a4 = w_all(w4in, me.zl, dev_zl)
    total_x(1, order[1])
    rings[3].mid()
    total_x(2, order[2])
    zring.start_near()
    w5in[me.zh] = w_sum(a4, w4in)
    a5 = w_all(w5in, me.zh, dev_zh)
    total_x(3, order[3])
    w6[me.y] = w_sum(a5, w5in)
    a6 = w_all(w6, me.y, dev_y)
    zring.mid()
    for one in a6:
        one.wait_recv()
    w7[me.x] = w6[...]
    a7 = w_all(w7, me.x, dev_x)
    for one in a7:
        one.wait_recv()
    gw_ref[me.core] = w7[...].reshape(T, F)
    a8 = net.copy(gw_ref.at[me.core], gw_ref.at[me.core], sib)
    for half in range(2):
        gx_ref[pl.ds(half * H, H)] = zring.total(half).astype(BF)
    a8.wait_recv()
    net.drain()


VM = pl.BlockSpec(memory_space=pltpu.VMEM)
SM = pl.BlockSpec(memory_space=pltpu.SMEM)
ANY = pl.BlockSpec(memory_space=pl.ANY)
DMA = pltpu.SemaphoreType.DMA


def shape(*dims, dtype=BF):
    return jax.ShapeDtypeStruct(dims, dtype)


def params(collective_id=None):
    if collective_id is None:
        return pltpu.CompilerParams(vmem_limit_bytes=48 * 2**20)
    return pltpu.CompilerParams(
        collective_id=collective_id, has_side_effects=True, vmem_limit_bytes=48 * 2**20
    )


def body(features, weight, grad_out, tiles, tile_rows, tile_cols, tile_count):
    slots = jnp.arange(128, dtype=jnp.int32)
    spot = jnp.where(slots < tile_count[0, 0], tile_rows[0, 0] * 32 + tile_cols[0, 0], -1)
    spots = jnp.arange(512, dtype=jnp.int32)
    place = jnp.min(jnp.where(spot[None, :] == spots[:, None], slots[None, :], 128), axis=1)

    x = pl.pallas_call(
        gather_x_kernel,
        out_shape=shape(4, 4, 2, T, F),
        in_specs=[VM],
        out_specs=VM,
        scratch_shapes=[DMA((40,)), DMA((40,))],
        compiler_params=params(0),
    )(features)
    part = pl.pallas_call(
        forward_kernel,
        out_shape=shape(2048, F),
        in_specs=[SM, ANY, VM],
        out_specs=VM,
        scratch_shapes=[pltpu.VMEM((129, T, T), BF), pltpu.VMEM((4, 2048, 1024), BF), DMA],
        compiler_params=params(),
    )(place, tiles.reshape(128, T, T), x.reshape(4, 1024, F))
    hidden, g, dw = pl.pallas_call(
        layer_kernel,
        out_shape=[shape(T, F), shape(4, 4, T, F), shape(F, F, dtype=F32)],
        in_specs=[VM] * 3,
        out_specs=[VM] * 3,
        scratch_shapes=[
            pltpu.VMEM((4, 2, 2, H, F), BF),
            pltpu.VMEM((4, 2, H, F), BF),
            pltpu.VMEM((4, 2, H, F), BF),
            pltpu.VMEM((3, T, F), BF),
            pltpu.VMEM((3, T, F), BF),
            DMA((60,)),
            DMA((60,)),
        ],
        compiler_params=params(1),
    )(part.reshape(4, 4, T, F), weight, grad_out)
    back = pl.pallas_call(
        backward_kernel,
        out_shape=shape(4096, F),
        in_specs=[SM, ANY, VM],
        out_specs=VM,
        scratch_shapes=[pltpu.VMEM((129, T, T), BF), pltpu.VMEM((4, 4096, 512), BF), DMA],
        compiler_params=params(),
    )(place, tiles.reshape(128, T, T), g.reshape(4, 512, F))
    grad_features, grad_weight = pl.pallas_call(
        scatter_kernel,
        out_shape=[shape(T, F), shape(2, T, F, dtype=F32)],
        in_specs=[VM] * 2,
        out_specs=[VM] * 2,
        scratch_shapes=[
            pltpu.VMEM((4, 4, T, F), BF),
            pltpu.VMEM((4, 4, T, F), BF),
            pltpu.VMEM((4, 2, 2, H, F), BF),
            pltpu.VMEM((4, 2, H, F), BF),
            pltpu.VMEM((4, 2, H, F), BF),
            pltpu.VMEM((4, T, F), BF),
            pltpu.VMEM((2, 2, H, F), BF),
            pltpu.VMEM((2, H, F), BF),
            pltpu.VMEM((2, H, F), BF),
            pltpu.VMEM((T, F), F32),
            pltpu.VMEM((T, F), F32),
            pltpu.VMEM((32, F), F32),
            pltpu.VMEM((3, 32, F), F32),
            pltpu.VMEM((8, F), F32),
            pltpu.VMEM((3, 8, F), F32),
            pltpu.VMEM((4, 8, F), F32),
            pltpu.VMEM((4, 8, F), F32),
            pltpu.VMEM((4, 8, F), F32),
            pltpu.VMEM((4, 4, 8, F), F32),
            DMA((60,)),
            DMA((60,)),
        ],
        compiler_params=params(2),
    )(back.reshape(4, 4, 2, T, F), dw)
    return hidden, grad_features, grad_weight.reshape(F, F)


def solution(mesh):
    return jax.shard_map(
        body,
        mesh=mesh,
        in_specs=(
            P(("col", "row"), None),
            P(),
            P(("row", "col"), None),
            P("row", "col", None, None, None),
            P("row", "col", None),
            P("row", "col", None),
            P("row", "col"),
        ),
        out_specs=(P(("row", "col"), None), P(("col", "row"), None), P()),
        check_vma=False,
    )
```

```python
import jax
import jax.numpy as jnp
from jax import lax
from jax.experimental import pallas as pl
from jax.experimental.pallas import tpu as pltpu
from jax.sharding import PartitionSpec as P

MESH = pl.DeviceIdType.MESH
BF = jnp.bfloat16
F32 = jnp.float32
root_half = 0.7071067811865476
inv_root_tau = 0.3989422804014327
T = 128
F = 256


class Place:
    def __init__(self):
        row, col = lax.axis_index("row"), lax.axis_index("col")
        self.zh, self.x, self.core = row // 8, (row // 2) % 4, row % 2
        self.zl, self.y = col // 4, col % 4
        self.z = self.zh * 4 + self.zl

    def at(self, zh=None, x=None, core=None, zl=None, y=None):
        zh = self.zh if zh is None else zh % 4
        x = self.x if x is None else x % 4
        core = self.core if core is None else core
        zl = self.zl if zl is None else zl % 4
        y = self.y if y is None else y % 4
        return ((zh * 4 + x) * 2 + core, zl * 4 + y)

    def along_z(self, d):
        z = (self.z + d) % 16
        return self.at(zh=z // 4, zl=z % 4)


class Net:
    def __init__(self, send, recv):
        self.send, self.recv, self.started = send, recv, []

    def copy(self, src, dst, device):
        n = len(self.started)
        one = pltpu.make_async_remote_copy(
            src_ref=src,
            dst_ref=dst,
            send_sem=self.send.at[n],
            recv_sem=self.recv.at[n],
            device_id=device,
            device_id_type=MESH,
        )
        one.start()
        self.started.append(one)
        return one

    def drain(self):
        for one in self.started:
            one.wait_send()


def meet(partners):
    barrier = pltpu.get_barrier_semaphore()
    for device in partners:
        pl.semaphore_signal(barrier, inc=1, device_id=device, device_id_type=MESH)
    pl.semaphore_wait(barrier, len(partners))


def rows_of(i, n):
    return pl.ds(pl.multiple_of(i * n, n), n)


def layer_kernel(
    place_ref, features_ref, w_hbm, go_hbm, tiles_ref,
    hid_ref, gx_ref, gw_ref,
    tilebuf, dense, turned, x_ref, acc, part, yland, zsum, zland, w_ref, go_ref, g_ref, dw_ref,
    acc2, back, cland, csum, xland, hsum, hland, w1, w1in, w2in, w4, local, send, recv,
):
    me = Place()
    net = Net(send, recv)
    zh, x, core, zl, y = me.zh, me.x, me.core, me.zl, me.y
    sib = me.at(core=1 - core)
    cross = [(e // 4, e % 4) for e in range(1, 16)]

    def fetch(src, dst, n):
        one = pltpu.make_async_copy(src, dst, local.at[n])
        one.start()
        return one

    own_in = fetch(features_ref, x_ref.at[zh, x, core], 0)
    tiles_in = fetch(tiles_ref, tilebuf.at[pl.ds(0, 128)], 1)
    w_in = fetch(w_hbm, w_ref, 2)
    go_in = fetch(go_hbm, go_ref, 3)
    meet(
        [sib]
        + [me.along_z(d) for d in range(1, 16)]
        + [me.at(x=x + dx, y=y + dy) for dx, dy in cross]
    )
    own_in.wait()

    def slot(a, b):
        return x_ref.at[a % 4, b % 4, core]

    over_z, over_x, over_c = {}, {}, {}
    for d in (2, 1, 3):
        over_z[d] = net.copy(slot(zh, x), slot(zh, x), me.at(zh=zh + d))

    def send_c(d, e):
        over_c[d, e] = net.copy(slot(zh - d, x - e), slot(zh - d, x - e), sib)

    def send_x(d):
        for e in (2, 1, 3):
            over_x[d, e] = net.copy(slot(zh - d, x), slot(zh - d, x), me.at(x=x + e))
        send_c(d, 0)

    def land_x(d):
        for e in (1, 3, 2):
            over_x[d, e].wait_recv()
            send_c(d, e)

    def land_c(d):
        for e in range(4):
            over_c[d, e].wait_recv()

    send_x(0)
    tilebuf[128] = jnp.zeros((T, T), BF)
    tiles_in.wait()

    def build(r, _):
        for c in range(32):
            dense[c // 8, rows_of(r, T), pl.ds((c % 8) * T, T)] = tilebuf[place_ref[r * 32 + c]]
        return 0

    lax.fori_loop(0, 16, build, 0)
    land_x(0)

    def forward(d, first):
        a = (zh - d) % 4
        xs = x_ref.at[a].reshape(1024, F)

        def block(m, _):
            more = jnp.dot(dense[a, rows_of(m, 512)], xs[...], preferred_element_type=F32)
            if first:
                acc[rows_of(m, 512)] = more
            else:
                acc[rows_of(m, 512)] += more
            return 0

        lax.fori_loop(0, 4, block, 0)

    over_z[1].wait_recv()
    send_x(1)
    over_z[3].wait_recv()
    send_x(3)
    land_c(0)
    forward(0, True)
    land_x(1)
    land_x(3)
    over_z[2].wait_recv()
    send_x(2)
    land_c(1)
    forward(1, False)
    land_c(3)
    forward(3, False)
    land_x(2)
    land_c(2)

    far = (zh + 2) % 4
    last_x = x_ref.at[far].reshape(1024, F)
    over_y = {}
    for d in (1, 2, 3, 0):
        q = (zl + d) % 4
        more = jnp.dot(dense[far, rows_of(q, 512)], last_x[...], preferred_element_type=F32)
        part[q] = (acc[rows_of(q, 512)] + more).astype(BF).reshape(4, T, F)
        for e in (2, 1, 3):
            over_y[d, e] = net.copy(part.at[q, (y + e) % 4], yland.at[d, e - 1], me.at(y=y + e))

    def turn(s, _):
        tilebuf[s] = tilebuf[s].T
        return 0

    over_l = {}
    for i, d in enumerate((1, 2, 3, 0)):
        lax.fori_loop(i * 32, i * 32 + 32, turn, 0)
        total = part[(zl + d) % 4, y].astype(F32)
        for e in (1, 3, 2):
            over_y[d, e].wait_recv()
            total += yland[d, e - 1].astype(F32)
        if d:
            zsum[d - 1] = total.astype(BF)
            over_l[d] = net.copy(zsum.at[d - 1], zland.at[d - 1], me.at(zl=zl + d))

    def build_back(k):
        def step(c, _):
            for j in range(4):
                turned[k, rows_of(c, T), pl.ds(j * T, T)] = tilebuf[place_ref[(k * 4 + j) * 32 + c]]
            return 0

        lax.fori_loop(0, 32, step, 0)

    build_back(zl)
    w_in.wait()
    go_in.wait()
    for d in (1, 2, 3):
        over_l[d].wait_recv()
        total += zland[d - 1].astype(F32)
    agg = total.astype(BF)

    w = w_ref[...]
    pre = jnp.dot(agg, w, preferred_element_type=F32)
    erf = lax.erf(pre * root_half)
    slope = 0.5 * (1.0 + erf) + pre * jnp.exp(-0.5 * pre * pre) * inv_root_tau
    pre_grad = (go_ref[...].astype(F32) * slope).astype(BF)
    prop = lax.dot_general(pre_grad, w, (((1,), (1,)), ((), ())), preferred_element_type=F32)
    g_ref[zl, y] = prop.astype(BF)

    def gslot(a, b):
        return g_ref.at[a % 4, b % 4]

    back_l, back_y = {}, {}
    for d in (3, 2, 1):
        back_l[d] = net.copy(gslot(zl, y), gslot(zl, y), me.at(zl=zl + d))

    def send_y(d):
        for e in (2, 1, 3):
            back_y[d, e] = net.copy(gslot(zl - d, y), gslot(zl - d, y), me.at(y=y + e))

    def land_y(d):
        for e in (1, 3, 2):
            back_y[d, e].wait_recv()

    send_y(0)
    hid_ref[...] = (0.5 * pre * (1.0 + erf)).astype(BF)
    dw_ref[...] = lax.dot_general(agg, pre_grad, (((0,), (0,)), ((), ())), preferred_element_type=F32)
    w_core = net.copy(dw_ref.at[rows_of(1 - core, T)], w1in, sib)
    build_back((zl + 3) % 4)
    for d in (1, 3, 2):
        back_l[d].wait_recv()
        send_y(d)

    w_core.wait_recv()
    w1[...] = dw_ref[rows_of(core, T)] + w1in[...]

    def piece(ref, dx, dy):
        return ref.at[rows_of((x + dx) % 4 * 4 + (y + dy) % 4, 8)]

    w_cross = [
        net.copy(piece(w1, dx, dy), w2in.at[dx * 4 + dy - 1], me.at(x=x + dx, y=y + dy))
        for dx, dy in cross
    ]
    build_back((zl + 1) % 4)

    def backward(d, first):
        a = (zl - d) % 4
        gs = g_ref.at[a].reshape(512, F)

        def block(m, _):
            more = jnp.dot(turned[a, rows_of(m, 512)], gs[...], preferred_element_type=F32)
            if first:
                acc2[rows_of(m, 512)] = more
            else:
                acc2[rows_of(m, 512)] += more
            return 0

        lax.fori_loop(0, 8, block, 0)

    build_back((zl + 2) % 4)
    land_y(0)
    backward(0, True)
    land_y(1)
    backward(1, False)
    for one in w_cross:
        one.wait_recv()
    total = piece(w1, 0, 0)[...]
    for e in range(15):
        total += w2in[e]
    w4[me.z] = total
    w_z = [net.copy(w4.at[me.z], w4.at[me.z], me.along_z(d)) for d in range(1, 16)]
    land_y(3)
    backward(3, False)
    land_y(2)

    last = (zl + 2) % 4
    last_g = g_ref.at[last].reshape(512, F)
    order = (2, 1, 3, 0)
    swaps, back_x, back_z = {}, {}, {}
    for d in order:
        q = (zh + d) % 4
        for half in range(2):
            m = q * 2 + half
            more = jnp.dot(turned[last, rows_of(m, 512)], last_g[...], preferred_element_type=F32)
            back[q, pl.ds(half * 2, 2)] = (
                (acc2[rows_of(m, 512)] + more).astype(BF).reshape(2, 2, T, F)
            )
        swaps[d] = net.copy(back.at[q, :, 1 - core], cland.at[d], sib)
    for d in order:
        q = (zh + d) % 4
        swaps[d].wait_recv()
        csum[d] = (back[q, :, core].astype(F32) + cland[d].astype(F32)).astype(BF)
        for e in (2, 1, 3):
            back_x[d, e] = net.copy(csum.at[d, (x + e) % 4], xland.at[d, e - 1], me.at(x=x + e))

    def land_back(d):
        total = csum[d, x].astype(F32)
        for e in (1, 3, 2):
            back_x[d, e].wait_recv()
            total += xland[d, e - 1].astype(F32)
        if d:
            hsum[d - 1] = total.astype(BF)
            back_z[d] = net.copy(hsum.at[d - 1], hland.at[d - 1], me.at(zh=zh + d))
        return total

    land_back(2)
    land_back(1)
    land_back(3)
    total = land_back(0)
    for one in w_z:
        one.wait_recv()
    mine = gw_ref.at[core, rows_of(x * 4 + y, 8)]
    mine[...] = jnp.sum(w4[...], axis=0)
    w_back = [net.copy(mine, mine, me.at(x=x + dx, y=y + dy)) for dx, dy in cross]
    for d in (1, 3):
        back_z[d].wait_recv()
        total += hland[d - 1].astype(F32)
    for one in w_back:
        one.wait_recv()
    w_last = net.copy(gw_ref.at[core], gw_ref.at[core], sib)
    back_z[2].wait_recv()
    gx_ref[...] = (total + hland[1].astype(F32)).astype(BF)
    w_last.wait_recv()
    net.drain()


VM = pl.BlockSpec(memory_space=pltpu.VMEM)
SM = pl.BlockSpec(memory_space=pltpu.SMEM)
ANY = pl.BlockSpec(memory_space=pl.ANY)
DMA = pltpu.SemaphoreType.DMA


def shape(*dims, dtype=BF):
    return jax.ShapeDtypeStruct(dims, dtype)


def body(features, weight, grad_out, tiles, tile_rows, tile_cols, tile_count):
    slots = jnp.arange(128, dtype=jnp.int32)
    spot = jnp.where(slots < tile_count[0, 0], tile_rows[0, 0] * 32 + tile_cols[0, 0], -1)
    spots = jnp.arange(512, dtype=jnp.int32)
    place = jnp.min(jnp.where(spot[None, :] == spots[:, None], slots[None, :], 128), axis=1)
    b16 = lambda *dims: pltpu.VMEM(dims, BF)
    b32 = lambda *dims: pltpu.VMEM(dims, F32)
    hidden, grad_features, grad_weight = pl.pallas_call(
        layer_kernel,
        out_shape=[shape(T, F), shape(T, F), shape(2, T, F, dtype=F32)],
        in_specs=[SM, ANY, ANY, ANY, ANY],
        out_specs=[VM] * 3,
        scratch_shapes=[
            b16(129, T, T),
            b16(4, 2048, 1024),
            b16(4, 4096, 512),
            b16(4, 4, 2, T, F),
            b32(2048, F),
            b16(4, 4, T, F),
            b16(4, 3, T, F),
            b16(3, T, F),
            b16(3, T, F),
            b16(F, F),
            b16(T, F),
            b16(4, 4, T, F),
            b32(F, F),
            b32(4096, F),
            b16(4, 4, 2, T, F),
            b16(4, 4, T, F),
            b16(4, 4, T, F),
            b16(4, 3, T, F),
            b16(3, T, F),
            b16(3, T, F),
            b32(T, F),
            b32(T, F),
            b32(15, 8, F),
            b32(16, 8, F),
            DMA((4,)),
            DMA((144,)),
            DMA((144,)),
        ],
        compiler_params=pltpu.CompilerParams(
            collective_id=0, has_side_effects=True, vmem_limit_bytes=60 * 2**20
        ),
    )(place, features, weight, grad_out, tiles.reshape(128, T, T))
    return hidden, grad_features, grad_weight.reshape(F, F)


def solution(mesh):
    return jax.shard_map(
        body,
        mesh=mesh,
        in_specs=(
            P(("col", "row"), None),
            P(),
            P(("row", "col"), None),
            P("row", "col", None, None, None),
            P("row", "col", None),
            P("row", "col", None),
            P("row", "col"),
        ),
        out_specs=(P(("row", "col"), None), P(("col", "row"), None), P()),
        check_vma=False,
    )
```

```python
import jax
import jax.numpy as jnp
from jax import lax
from jax.experimental import pallas as pl
from jax.experimental.pallas import tpu as pltpu
from jax.sharding import PartitionSpec as P

MESH = pl.DeviceIdType.MESH
BF = jnp.bfloat16
F32 = jnp.float32
root_half = 0.7071067811865476
inv_root_tau = 0.3989422804014327
T = 128
F = 256


class Place:
    def __init__(self):
        row, col = lax.axis_index("row"), lax.axis_index("col")
        self.zh, self.x, self.core = row // 8, (row // 2) % 4, row % 2
        self.zl, self.y = col // 4, col % 4
        self.z = self.zh * 4 + self.zl

    def at(self, zh=None, x=None, core=None, zl=None, y=None):
        zh = self.zh if zh is None else zh % 4
        x = self.x if x is None else x % 4
        core = self.core if core is None else core
        zl = self.zl if zl is None else zl % 4
        y = self.y if y is None else y % 4
        return ((zh * 4 + x) * 2 + core, zl * 4 + y)

    def along_z(self, d):
        z = (self.z + d) % 16
        return self.at(zh=z // 4, zl=z % 4)


class Net:
    def __init__(self, send, recv):
        self.send, self.recv, self.started = send, recv, []

    def copy(self, src, dst, device):
        n = len(self.started)
        one = pltpu.make_async_remote_copy(
            src_ref=src,
            dst_ref=dst,
            send_sem=self.send.at[n],
            recv_sem=self.recv.at[n],
            device_id=device,
            device_id_type=MESH,
        )
        one.start()
        self.started.append(one)
        return one

    def drain(self):
        for one in self.started:
            one.wait_send()


def meet(partners):
    barrier = pltpu.get_barrier_semaphore()
    for device in partners:
        pl.semaphore_signal(barrier, inc=1, device_id=device, device_id_type=MESH)
    pl.semaphore_wait(barrier, len(partners))


def rows_of(i, n):
    return pl.ds(pl.multiple_of(i * n, n), n)


def layer_kernel(
    count_ref, rows_hbm, cols_hbm, features_ref, w_hbm, go_hbm, tiles_ref,
    hid_ref, gx_ref, gw_ref,
    tilebuf, dense, turned, x_ref, acc, part, yland, zsum, zland, w_ref, go_ref, g_ref, dw_ref,
    acc2, back, cland, csum, xland, hsum, hland, w1, w1in, w2in, w4, spots, place_vm, place_ref,
    local, send, recv,
):
    me = Place()
    net = Net(send, recv)
    zh, x, core, zl, y = me.zh, me.x, me.core, me.zl, me.y
    sib = me.at(core=1 - core)
    cross = [(e // 4, e % 4) for e in range(1, 16)]

    def fetch(src, dst, n):
        one = pltpu.make_async_copy(src, dst, local.at[n])
        one.start()
        return one

    own_in = fetch(features_ref, x_ref.at[zh, x, core], 0)
    rows_in = fetch(rows_hbm, spots.at[0], 4)
    cols_in = fetch(cols_hbm, spots.at[1], 5)
    tiles_in = fetch(tiles_ref, tilebuf.at[pl.ds(0, 128)], 1)
    w_in = fetch(w_hbm, w_ref, 2)
    go_in = fetch(go_hbm, go_ref, 3)
    meet(
        [sib, me.at(zh=zh + 1), me.at(zh=zh - 1)]
        + [me.at(x=x + d) for d in (1, 2, 3)]
        + [me.at(y=y + d) for d in (1, 2, 3)]
        + [me.at(zl=zl + d) for d in (1, 2, 3)]
    )
    own_in.wait()

    def slot(a, b):
        return x_ref.at[a % 4, b % 4, core]

    over_z, over_x, over_c = {}, {}, {}
    for d in (1, 3):
        over_z[d] = net.copy(slot(zh, x), slot(zh, x), me.at(zh=zh + d))

    def pass_on(d, half):
        part_of = slot(zh - d, x).at[pl.ds(half * 64, 64)]
        over_z[d, half] = net.copy(part_of, part_of, me.at(zh=zh + d))

    def send_c(d, e):
        over_c[d, e] = net.copy(slot(zh - d, x - e), slot(zh - d, x - e), sib)

    def send_x(d):
        for e in (2, 1, 3):
            over_x[d, e] = net.copy(slot(zh - d, x), slot(zh - d, x), me.at(x=x + e))
        send_c(d, 0)

    def land_x(d):
        for e in (1, 3, 2):
            over_x[d, e].wait_recv()
            send_c(d, e)

    def land_c(d):
        for e in range(4):
            over_c[d, e].wait_recv()

    send_x(0)

    rows_in.wait()
    cols_in.wait()
    lane = lax.broadcasted_iota(jnp.int32, (T, T), 1)
    slot_id = lax.broadcasted_iota(jnp.int32, (T, T), 0)
    spot = jnp.where(lane < count_ref[0, 0], spots[0] * 32 + spots[1], -1)
    spot = jnp.sum(jnp.where(lane == slot_id, spot, 0), axis=1, keepdims=True)
    hit = spot == lax.broadcasted_iota(jnp.int32, (T, 512), 1)
    found = jnp.where(hit, lax.broadcasted_iota(jnp.int32, (T, 512), 0) - 128, 0)
    place_vm[...] = jnp.sum(found, axis=0, keepdims=True) + 128
    place_in = fetch(place_vm, place_ref, 6)
    tilebuf[128] = jnp.zeros((T, T), BF)
    tiles_in.wait()
    place_in.wait()

    def build(r, _):
        for c in range(32):
            dense[c // 8, rows_of(r, T), pl.ds((c % 8) * T, T)] = tilebuf[place_ref[0, r * 32 + c]]
        return 0

    lax.fori_loop(0, 16, build, 0)
    land_x(0)

    def forward(d, first):
        a = (zh - d) % 4
        xs = x_ref.at[a].reshape(1024, F)

        def block(m, _):
            more = jnp.dot(dense[a, rows_of(m, 512)], xs[...], preferred_element_type=F32)
            if first:
                acc[rows_of(m, 512)] = more
            else:
                acc[rows_of(m, 512)] += more
            return 0

        lax.fori_loop(0, 4, block, 0)

    over_z[1].wait_recv()
    pass_on(1, 0)
    send_x(1)
    over_z[3].wait_recv()
    pass_on(3, 1)
    send_x(3)
    land_c(0)
    forward(0, True)
    land_x(1)
    land_x(3)
    over_z[1, 0].wait_recv()
    over_z[3, 1].wait_recv()
    send_x(2)
    land_c(1)
    forward(1, False)
    land_c(3)
    forward(3, False)
    land_x(2)
    land_c(2)

    far = (zh + 2) % 4
    last_x = x_ref.at[far].reshape(1024, F)
    over_y = {}
    for d in (1, 2, 3, 0):
        q = (zl + d) % 4
        more = jnp.dot(dense[far, rows_of(q, 512)], last_x[...], preferred_element_type=F32)
        part[q] = (acc[rows_of(q, 512)] + more).astype(BF).reshape(4, T, F)
        for e in (2, 1, 3):
            over_y[d, e] = net.copy(part.at[q, (y + e) % 4], yland.at[d, e - 1], me.at(y=y + e))

    def turn(s, _):
        tilebuf[s] = tilebuf[s].T
        return 0

    over_l = {}
    for i, d in enumerate((1, 2, 3, 0)):
        lax.fori_loop(i * 32, i * 32 + 32, turn, 0)
        total = part[(zl + d) % 4, y].astype(F32)
        for e in (1, 3, 2):
            over_y[d, e].wait_recv()
            total += yland[d, e - 1].astype(F32)
        if d:
            zsum[d - 1] = total.astype(BF)
            over_l[d] = net.copy(zsum.at[d - 1], zland.at[d - 1], me.at(zl=zl + d))

    def build_back(k):
        def step(c, _):
            for j in range(4):
                turned[k, rows_of(c, T), pl.ds(j * T, T)] = tilebuf[place_ref[0, (k * 4 + j) * 32 + c]]
            return 0

        lax.fori_loop(0, 32, step, 0)

    build_back(zl)
    w_in.wait()
    go_in.wait()
    for d in (1, 2, 3):
        over_l[d].wait_recv()
        total += zland[d - 1].astype(F32)
    agg = total.astype(BF)

    w = w_ref[...]
    pre = jnp.dot(agg, w, preferred_element_type=F32)
    erf = lax.erf(pre * root_half)
    slope = 0.5 * (1.0 + erf) + pre * jnp.exp(-0.5 * pre * pre) * inv_root_tau
    pre_grad = (go_ref[...].astype(F32) * slope).astype(BF)
    prop = lax.dot_general(pre_grad, w, (((1,), (1,)), ((), ())), preferred_element_type=F32)
    g_ref[zl, y] = prop.astype(BF)

    def gslot(a, b):
        return g_ref.at[a % 4, b % 4]

    back_l, back_y = {}, {}
    for d in (3, 2, 1):
        back_l[d] = net.copy(gslot(zl, y), gslot(zl, y), me.at(zl=zl + d))

    def send_y(d):
        for e in (2, 1, 3):
            back_y[d, e] = net.copy(gslot(zl - d, y), gslot(zl - d, y), me.at(y=y + e))

    def land_y(d):
        for e in (1, 3, 2):
            back_y[d, e].wait_recv()

    send_y(0)
    hid_ref[...] = (0.5 * pre * (1.0 + erf)).astype(BF)
    dw_ref[...] = lax.dot_general(agg, pre_grad, (((0,), (0,)), ((), ())), preferred_element_type=F32)
    w_core = net.copy(dw_ref.at[rows_of(1 - core, T)], w1in, sib)
    build_back((zl + 3) % 4)
    for d in (1, 3, 2):
        back_l[d].wait_recv()
        send_y(d)

    w_core.wait_recv()
    w1[...] = dw_ref[rows_of(core, T)] + w1in[...]

    def piece(ref, dx, dy):
        return ref.at[rows_of((x + dx) % 4 * 4 + (y + dy) % 4, 8)]

    w_cross = [
        net.copy(piece(w1, dx, dy), w2in.at[dx * 4 + dy - 1], me.at(x=x + dx, y=y + dy))
        for dx, dy in cross
    ]
    build_back((zl + 1) % 4)

    def backward(d, first):
        a = (zl - d) % 4
        gs = g_ref.at[a].reshape(512, F)

        def block(m, _):
            more = jnp.dot(turned[a, rows_of(m, 512)], gs[...], preferred_element_type=F32)
            if first:
                acc2[rows_of(m, 512)] = more
            else:
                acc2[rows_of(m, 512)] += more
            return 0

        lax.fori_loop(0, 8, block, 0)

    build_back((zl + 2) % 4)
    land_y(0)
    backward(0, True)
    land_y(1)
    backward(1, False)
    for one in w_cross:
        one.wait_recv()
    total = piece(w1, 0, 0)[...]
    for e in range(15):
        total += w2in[e]
    w4[me.z] = total
    w_z = [net.copy(w4.at[me.z], w4.at[me.z], me.along_z(d)) for d in range(1, 16)]
    land_y(3)
    backward(3, False)
    land_y(2)

    last = (zl + 2) % 4
    last_g = g_ref.at[last].reshape(512, F)
    order = (2, 1, 3, 0)
    swaps, back_x, back_z = {}, {}, {}
    for d in order:
        q = (zh + d) % 4
        for half in range(2):
            m = q * 2 + half
            more = jnp.dot(turned[last, rows_of(m, 512)], last_g[...], preferred_element_type=F32)
            back[q, pl.ds(half * 2, 2)] = (
                (acc2[rows_of(m, 512)] + more).astype(BF).reshape(2, 2, T, F)
            )
        swaps[d] = net.copy(back.at[q, :, 1 - core], cland.at[d], sib)
    for d in order:
        q = (zh + d) % 4
        swaps[d].wait_recv()
        csum[d] = (back[q, :, core].astype(F32) + cland[d].astype(F32)).astype(BF)
        for e in (2, 1, 3):
            back_x[d, e] = net.copy(csum.at[d, (x + e) % 4], xland.at[d, e - 1], me.at(x=x + e))

    def land_back(d):
        total = csum[d, x].astype(F32)
        for e in (1, 3, 2):
            back_x[d, e].wait_recv()
            total += xland[d, e - 1].astype(F32)
        if d:
            hsum[d - 1] = total.astype(BF)
            back_z[d] = net.copy(hsum.at[d - 1], hland.at[d - 1], me.at(zh=zh + d))
        return total

    land_back(2)
    for one in w_z:
        one.wait_recv()
    mine = gw_ref.at[core, rows_of(x * 4 + y, 8)]
    mine[...] = jnp.sum(w4[...], axis=0)
    w_back = [net.copy(mine, mine, me.at(x=x + dx, y=y + dy)) for dx, dy in cross]
    land_back(1)
    land_back(3)
    total = land_back(0)
    for one in w_back:
        one.wait_recv()
    w_last = net.copy(gw_ref.at[core], gw_ref.at[core], sib)
    for d in (1, 3):
        back_z[d].wait_recv()
        total += hland[d - 1].astype(F32)
    back_z[2].wait_recv()
    gx_ref[...] = (total + hland[1].astype(F32)).astype(BF)
    w_last.wait_recv()
    net.drain()


VM = pl.BlockSpec(memory_space=pltpu.VMEM)
SM = pl.BlockSpec(memory_space=pltpu.SMEM)
ANY = pl.BlockSpec(memory_space=pl.ANY)
DMA = pltpu.SemaphoreType.DMA


def shape(*dims, dtype=BF):
    return jax.ShapeDtypeStruct(dims, dtype)


def hand_over_kernel(a_ref, b_ref, c_ref, a_out, b_out, c_out, a_mid, b_mid, c_mid, sems):
    triples = ((a_ref, a_mid, a_out), (b_ref, b_mid, b_out), (c_ref, c_mid, c_out))
    inward = [pltpu.make_async_copy(src, mid, sems.at[0, n]) for n, (src, mid, _) in enumerate(triples)]
    outward = [pltpu.make_async_copy(mid, dst, sems.at[1, n]) for n, (_, mid, dst) in enumerate(triples)]
    for one in inward:
        one.start()
    for one, other in zip(inward, outward):
        one.wait()
        other.start()
    for one in outward:
        one.wait()


def body(features, weight, grad_out, tiles, tile_rows, tile_cols, tile_count):
    b16 = lambda *dims: pltpu.VMEM(dims, BF)
    b32 = lambda *dims: pltpu.VMEM(dims, F32)
    found = pl.pallas_call(
        layer_kernel,
        out_shape=[shape(T, F), shape(T, F), shape(2, T, F, dtype=F32)],
        in_specs=[SM] + [ANY] * 6,
        out_specs=[VM] * 3,
        scratch_shapes=[
            b16(129, T, T),
            b16(4, 2048, 1024),
            b16(4, 4096, 512),
            b16(4, 4, 2, T, F),
            b32(2048, F),
            b16(4, 4, T, F),
            b16(4, 3, T, F),
            b16(3, T, F),
            b16(3, T, F),
            b16(F, F),
            b16(T, F),
            b16(4, 4, T, F),
            b32(F, F),
            b32(4096, F),
            b16(4, 4, 2, T, F),
            b16(4, 4, T, F),
            b16(4, 4, T, F),
            b16(4, 3, T, F),
            b16(3, T, F),
            b16(3, T, F),
            b32(T, F),
            b32(T, F),
            b32(15, 8, F),
            b32(16, 8, F),
            pltpu.VMEM((2, 1, T), jnp.int32),
            pltpu.VMEM((1, 512), jnp.int32),
            pltpu.SMEM((1, 512), jnp.int32),
            DMA((8,)),
            DMA((144,)),
            DMA((144,)),
        ],
        compiler_params=pltpu.CompilerParams(
            collective_id=0, has_side_effects=True, vmem_limit_bytes=60 * 2**20
        ),
    )(
        tile_count,
        tile_rows.reshape(1, T),
        tile_cols.reshape(1, T),
        features,
        weight,
        grad_out,
        tiles.reshape(128, T, T),
    )
    hidden, grad_features, grad_weight = pl.pallas_call(
        hand_over_kernel,
        out_shape=[shape(T, F), shape(T, F), shape(2, T, F, dtype=F32)],
        in_specs=[ANY] * 3,
        out_specs=[ANY] * 3,
        scratch_shapes=[b16(T, F), b16(T, F), b32(2, T, F), DMA((2, 3))],
    )(*found)
    return hidden, grad_features, grad_weight.reshape(F, F)


def solution(mesh):
    return jax.shard_map(
        body,
        mesh=mesh,
        in_specs=(
            P(("col", "row"), None),
            P(),
            P(("row", "col"), None),
            P("row", "col", None, None, None),
            P("row", "col", None),
            P("row", "col", None),
            P("row", "col"),
        ),
        out_specs=(P(("row", "col"), None), P(("col", "row"), None), P()),
        check_vma=False,
    )
```

```python
import jax
import jax.numpy as jnp
from jax import lax
from jax.experimental import pallas as pl
from jax.experimental.pallas import tpu as pltpu
from jax.sharding import PartitionSpec as P

MESH = pl.DeviceIdType.MESH
BF = jnp.bfloat16
F32 = jnp.float32
root_half = 0.7071067811865476
inv_root_tau = 0.3989422804014327
T = 128
F = 256


class Place:
    def __init__(self):
        row, col = lax.axis_index("row"), lax.axis_index("col")
        self.zh, self.x, self.core = row // 8, (row // 2) % 4, row % 2
        self.zl, self.y = col // 4, col % 4
        self.z = self.zh * 4 + self.zl

    def at(self, zh=None, x=None, core=None, zl=None, y=None):
        zh = self.zh if zh is None else zh % 4
        x = self.x if x is None else x % 4
        core = self.core if core is None else core
        zl = self.zl if zl is None else zl % 4
        y = self.y if y is None else y % 4
        return ((zh * 4 + x) * 2 + core, zl * 4 + y)

    def along_z(self, d):
        z = (self.z + d) % 16
        return self.at(zh=z // 4, zl=z % 4)


class Net:
    def __init__(self, send, recv):
        self.send, self.recv, self.started = send, recv, []

    def copy(self, src, dst, device):
        n = len(self.started)
        one = pltpu.make_async_remote_copy(
            src_ref=src,
            dst_ref=dst,
            send_sem=self.send.at[n],
            recv_sem=self.recv.at[n],
            device_id=device,
            device_id_type=MESH,
        )
        one.start()
        self.started.append(one)
        return one

    def drain(self):
        for one in self.started:
            one.wait_send()


def meet(partners):
    barrier = pltpu.get_barrier_semaphore()
    for device in partners:
        pl.semaphore_signal(barrier, inc=1, device_id=device, device_id_type=MESH)
    pl.semaphore_wait(barrier, len(partners))


def rows_of(i, n):
    return pl.ds(pl.multiple_of(i * n, n), n)


def layer_kernel(
    count_hbm, rows_hbm, cols_hbm, features_ref, w_hbm, go_hbm, tiles_ref,
    hid_ref, gx_ref, gw_ref,
    tilebuf, dense, turned, x_ref, acc, part, yland, zsum, zland, w_ref, wt_ref, go_ref, g_ref, dw_ref,
    acc2, back, cland, csum, xland, hsum, hland, w1, w1in, w2in, w4, spots, place_vm, place_ref, count_ref,
    local, send, recv,
):
    me = Place()
    net = Net(send, recv)
    zh, x, core, zl, y = me.zh, me.x, me.core, me.zl, me.y
    sib = me.at(core=1 - core)
    cross = [(e // 4, e % 4) for e in range(1, 16)]

    def fetch(src, dst, n):
        one = pltpu.make_async_copy(src, dst, local.at[n])
        one.start()
        return one

    own_in = fetch(features_ref, x_ref.at[zh, x, core], 0)
    count_in = fetch(count_hbm, count_ref, 7)
    rows_in = fetch(rows_hbm, spots.at[0], 4)
    cols_in = fetch(cols_hbm, spots.at[1], 5)
    tiles_in = fetch(tiles_ref, tilebuf.at[pl.ds(0, 128)], 1)
    w_in = fetch(w_hbm, w_ref, 2)
    go_in = fetch(go_hbm, go_ref, 3)
    meet(
        [sib, me.at(zh=zh + 1), me.at(zh=zh - 1)]
        + [me.at(x=x + d) for d in (1, 2, 3)]
        + [me.at(y=y + d) for d in (1, 2, 3)]
        + [me.at(zl=zl + d) for d in (1, 2, 3)]
    )
    own_in.wait()

    def slot(a, b):
        return x_ref.at[a % 4, b % 4, core]

    over_z, over_x, over_c = {}, {}, {}
    for d in (1, 3):
        over_z[d] = net.copy(slot(zh, x), slot(zh, x), me.at(zh=zh + d))

    def pass_on(d, half):
        part_of = slot(zh - d, x).at[pl.ds(half * 64, 64)]
        over_z[d, half] = net.copy(part_of, part_of, me.at(zh=zh + d))

    def send_c(d, e):
        over_c[d, e] = net.copy(slot(zh - d, x - e), slot(zh - d, x - e), sib)

    def send_x(d):
        for e in (2, 1, 3):
            over_x[d, e] = net.copy(slot(zh - d, x), slot(zh - d, x), me.at(x=x + e))
        send_c(d, 0)

    def land_x(d):
        for e in (1, 3, 2):
            over_x[d, e].wait_recv()
            send_c(d, e)

    def land_c(d):
        for e in range(4):
            over_c[d, e].wait_recv()

    send_x(0)

    count_in.wait()
    rows_in.wait()
    cols_in.wait()
    lane = lax.broadcasted_iota(jnp.int32, (T, T), 1)
    slot_id = lax.broadcasted_iota(jnp.int32, (T, T), 0)
    spot = jnp.where(lane < count_ref[0, 0], spots[0] * 32 + spots[1], -1)
    spot = jnp.sum(jnp.where(lane == slot_id, spot, 0), axis=1, keepdims=True)
    hit = spot == lax.broadcasted_iota(jnp.int32, (T, 512), 1)
    found = jnp.where(hit, lax.broadcasted_iota(jnp.int32, (T, 512), 0) - 128, 0)
    place_vm[...] = jnp.sum(found, axis=0, keepdims=True) + 128
    place_in = fetch(place_vm, place_ref, 6)
    tilebuf[128] = jnp.zeros((T, T), BF)
    tiles_in.wait()
    place_in.wait()

    def build(r, _):
        for c in range(32):
            dense[c // 8, rows_of(r, T), pl.ds((c % 8) * T, T)] = tilebuf[place_ref[0, r * 32 + c]]
        return 0

    lax.fori_loop(0, 16, build, 0)
    land_x(0)

    def turn(s, _):
        for j in range(8):
            tilebuf[s * 8 + j] = tilebuf[s * 8 + j].T
        return 0

    def build_back(k):
        def step(c, _):
            for j in range(4):
                turned[k, rows_of(c, T), pl.ds(j * T, T)] = tilebuf[place_ref[0, (k * 4 + j) * 32 + c]]
            return 0

        lax.fori_loop(0, 32, step, 0)

    lax.fori_loop(0, 16, turn, 0)

    def forward(d, first):
        a = (zh - d) % 4
        xs = x_ref.at[a].reshape(1024, F)

        def block(m, _):
            more = jnp.dot(dense[a, rows_of(m, 1024)], xs[...], preferred_element_type=F32)
            if first:
                acc[rows_of(m, 1024)] = more
            else:
                acc[rows_of(m, 1024)] += more
            return 0

        lax.fori_loop(0, 2, block, 0)

    over_z[1].wait_recv()
    pass_on(1, 0)
    send_x(1)
    over_z[3].wait_recv()
    pass_on(3, 1)
    send_x(3)
    land_c(0)
    forward(0, True)
    build_back((zl + 3) % 4)
    land_x(1)
    land_x(3)
    over_z[1, 0].wait_recv()
    over_z[3, 1].wait_recv()
    send_x(2)
    land_c(1)
    forward(1, False)
    land_c(3)
    forward(3, False)
    land_x(2)
    land_c(2)

    far = (zh + 2) % 4
    last_x = x_ref.at[far].reshape(1024, F)
    over_y = {}
    for d in (1, 2, 3, 0):
        q = (zl + d) % 4
        more = jnp.dot(dense[far, rows_of(q, 512)], last_x[...], preferred_element_type=F32)
        part[q] = (acc[rows_of(q, 512)] + more).astype(BF).reshape(4, T, F)
        for e in (2, 1, 3):
            over_y[d, e] = net.copy(part.at[q, (y + e) % 4], yland.at[d, e - 1], me.at(y=y + e))

    over_l = {}
    for d in (1, 2, 3, 0):
        if d != 1:
            build_back((zl + 4 - d) % 4)
        total = part[(zl + d) % 4, y].astype(F32)
        for e in (1, 3, 2):
            over_y[d, e].wait_recv()
            total += yland[d, e - 1].astype(F32)
        if d:
            zsum[d - 1] = total.astype(BF)
            over_l[d] = net.copy(zsum.at[d - 1], zland.at[d - 1], me.at(zl=zl + d))

    w_in.wait()
    wt_ref[...] = w_ref[...].T
    go_in.wait()
    for d in (1, 2, 3):
        over_l[d].wait_recv()
        total += zland[d - 1].astype(F32)
    agg = total.astype(BF)

    w = w_ref[...]
    pre = jnp.dot(agg, w, preferred_element_type=F32)
    erf = lax.erf(pre * root_half)
    slope = 0.5 * (1.0 + erf) + pre * jnp.exp(-0.5 * pre * pre) * inv_root_tau
    pre_grad = (go_ref[...].astype(F32) * slope).astype(BF)
    prop = jnp.dot(pre_grad, wt_ref[...], preferred_element_type=F32)
    g_ref[zl, y] = prop.astype(BF)

    def gslot(a, b):
        return g_ref.at[a % 4, b % 4]

    back_l, back_y = {}, {}
    for d in (3, 2, 1):
        back_l[d] = net.copy(gslot(zl, y), gslot(zl, y), me.at(zl=zl + d))

    def send_y(d):
        for e in (2, 1, 3):
            back_y[d, e] = net.copy(gslot(zl - d, y), gslot(zl - d, y), me.at(y=y + e))

    def land_y(d):
        for e in (1, 3, 2):
            back_y[d, e].wait_recv()

    send_y(0)
    hid_ref[...] = (0.5 * pre * (1.0 + erf)).astype(BF)
    dw_ref[...] = lax.dot_general(agg, pre_grad, (((0,), (0,)), ((), ())), preferred_element_type=F32)
    w_core = net.copy(dw_ref.at[rows_of(1 - core, T)], w1in, sib)

    w_core.wait_recv()
    w1[...] = dw_ref[rows_of(core, T)] + w1in[...]

    def piece(ref, dx, dy):
        return ref.at[rows_of((x + dx) % 4 * 4 + (y + dy) % 4, 8)]

    w_cross = [
        net.copy(piece(w1, dx, dy), w2in.at[dx * 4 + dy - 1], me.at(x=x + dx, y=y + dy))
        for dx, dy in cross
    ]
    for d in (1, 3, 2):
        back_l[d].wait_recv()
        send_y(d)

    def backward(d, first):
        a = (zl - d) % 4
        gs = g_ref.at[a].reshape(512, F)

        def block(m, _):
            more = jnp.dot(turned[a, rows_of(m, 2048)], gs[...], preferred_element_type=F32)
            if first:
                acc2[rows_of(m, 2048)] = more
            else:
                acc2[rows_of(m, 2048)] += more
            return 0

        lax.fori_loop(0, 2, block, 0)

    land_y(0)
    backward(0, True)
    for one in w_cross:
        one.wait_recv()
    total = piece(w1, 0, 0)[...]
    for e in range(15):
        total += w2in[e]
    w4[me.z] = total
    w_z = [net.copy(w4.at[me.z], w4.at[me.z], me.along_z(d)) for d in range(1, 16)]
    land_y(1)
    backward(1, False)
    land_y(3)
    backward(3, False)
    land_y(2)

    last = (zl + 2) % 4
    last_g = g_ref.at[last].reshape(512, F)
    order = (2, 1, 3, 0)
    swaps, back_x, back_z = {}, {}, {}
    for d in order:
        q = (zh + d) % 4
        more = jnp.dot(turned[last, rows_of(q, 1024)], last_g[...], preferred_element_type=F32)
        back[q] = (acc2[rows_of(q, 1024)] + more).astype(BF).reshape(4, 2, T, F)
        swaps[d] = net.copy(back.at[q, :, 1 - core], cland.at[d], sib)
    for d in order:
        q = (zh + d) % 4
        swaps[d].wait_recv()
        csum[d] = (back[q, :, core].astype(F32) + cland[d].astype(F32)).astype(BF)
        for e in (2, 1, 3):
            back_x[d, e] = net.copy(csum.at[d, (x + e) % 4], xland.at[d, e - 1], me.at(x=x + e))

    def land_back(d):
        total = csum[d, x].astype(F32)
        for e in (1, 3, 2):
            back_x[d, e].wait_recv()
            total += xland[d, e - 1].astype(F32)
        if d:
            hsum[d - 1] = total.astype(BF)
            back_z[d] = net.copy(hsum.at[d - 1], hland.at[d - 1], me.at(zh=zh + d))
        return total

    land_back(2)
    land_back(1)
    land_back(3)
    for one in w_z:
        one.wait_recv()
    mine = gw_ref.at[core, rows_of(x * 4 + y, 8)]
    mine[...] = jnp.sum(w4[...], axis=0)
    w_back = [net.copy(mine, mine, me.at(x=x + dx, y=y + dy)) for dx, dy in cross]
    total = land_back(0)
    for one in w_back:
        one.wait_recv()
    w_last = net.copy(gw_ref.at[core], gw_ref.at[core], sib)
    for d in (1, 3):
        back_z[d].wait_recv()
        total += hland[d - 1].astype(F32)
    back_z[2].wait_recv()
    gx_ref[...] = (total + hland[1].astype(F32)).astype(BF)
    w_last.wait_recv()
    net.drain()


VM = pl.BlockSpec(memory_space=pltpu.VMEM)
ANY = pl.BlockSpec(memory_space=pl.ANY)
DMA = pltpu.SemaphoreType.DMA


def shape(*dims, dtype=BF):
    return jax.ShapeDtypeStruct(dims, dtype)


def hand_over_kernel(a_ref, b_ref, c_ref, a_out, b_out, c_out, a_mid, b_mid, c_mid, sems):
    triples = ((a_ref, a_mid, a_out), (b_ref, b_mid, b_out), (c_ref, c_mid, c_out))
    inward = [pltpu.make_async_copy(src, mid, sems.at[0, n]) for n, (src, mid, _) in enumerate(triples)]
    outward = [pltpu.make_async_copy(mid, dst, sems.at[1, n]) for n, (_, mid, dst) in enumerate(triples)]
    for one in inward:
        one.start()
    for one, other in zip(inward, outward):
        one.wait()
        other.start()
    for one in outward:
        one.wait()


def body(features, weight, grad_out, tiles, tile_rows, tile_cols, tile_count):
    b16 = lambda *dims: pltpu.VMEM(dims, BF)
    b32 = lambda *dims: pltpu.VMEM(dims, F32)
    found = pl.pallas_call(
        layer_kernel,
        out_shape=[shape(T, F), shape(T, F), shape(2, T, F, dtype=F32)],
        in_specs=[ANY] * 7,
        out_specs=[VM] * 3,
        scratch_shapes=[
            b16(129, T, T),
            b16(4, 2048, 1024),
            b16(4, 4096, 512),
            b16(4, 4, 2, T, F),
            b32(2048, F),
            b16(4, 4, T, F),
            b16(4, 3, T, F),
            b16(3, T, F),
            b16(3, T, F),
            b16(F, F),
            b16(F, F),
            b16(T, F),
            b16(4, 4, T, F),
            b32(F, F),
            b32(4096, F),
            b16(4, 4, 2, T, F),
            b16(4, 4, T, F),
            b16(4, 4, T, F),
            b16(4, 3, T, F),
            b16(3, T, F),
            b16(3, T, F),
            b32(T, F),
            b32(T, F),
            b32(15, 8, F),
            b32(16, 8, F),
            pltpu.VMEM((2, 1, T), jnp.int32),
            pltpu.VMEM((1, 512), jnp.int32),
            pltpu.SMEM((1, 512), jnp.int32),
            pltpu.SMEM((1, 1), jnp.int32),
            DMA((8,)),
            DMA((144,)),
            DMA((144,)),
        ],
        compiler_params=pltpu.CompilerParams(
            collective_id=0, has_side_effects=True, vmem_limit_bytes=57 * 2**20
        ),
    )(
        tile_count,
        tile_rows.reshape(1, T),
        tile_cols.reshape(1, T),
        features,
        weight,
        grad_out,
        tiles.reshape(128, T, T),
    )
    hidden, grad_features, grad_weight = pl.pallas_call(
        hand_over_kernel,
        out_shape=[shape(T, F), shape(T, F), shape(2, T, F, dtype=F32)],
        in_specs=[ANY] * 3,
        out_specs=[ANY] * 3,
        scratch_shapes=[b16(T, F), b16(T, F), b32(2, T, F), DMA((2, 3))],
    )(*found)
    return hidden, grad_features, grad_weight.reshape(F, F)


def solution(mesh):
    return jax.shard_map(
        body,
        mesh=mesh,
        in_specs=(
            P(("col", "row"), None),
            P(),
            P(("row", "col"), None),
            P("row", "col", None, None, None),
            P("row", "col", None),
            P("row", "col", None),
            P("row", "col"),
        ),
        out_specs=(P(("row", "col"), None), P(("col", "row"), None), P()),
        check_vma=False,
    )
```

```python
import jax
import jax.numpy as jnp
from jax import lax
from jax.experimental import pallas as pl
from jax.experimental.pallas import tpu as pltpu
from jax.sharding import PartitionSpec as P

MESH = pl.DeviceIdType.MESH
BF = jnp.bfloat16
F32 = jnp.float32
root_half = 0.7071067811865476
inv_root_tau = 0.3989422804014327
T = 128
F = 256


class Place:
    def __init__(self):
        row, col = lax.axis_index("row"), lax.axis_index("col")
        self.zh, self.x, self.core = row // 8, (row // 2) % 4, row % 2
        self.zl, self.y = col // 4, col % 4
        self.z = self.zh * 4 + self.zl

    def at(self, zh=None, x=None, core=None, zl=None, y=None):
        zh = self.zh if zh is None else zh % 4
        x = self.x if x is None else x % 4
        core = self.core if core is None else core
        zl = self.zl if zl is None else zl % 4
        y = self.y if y is None else y % 4
        return ((zh * 4 + x) * 2 + core, zl * 4 + y)

    def along_z(self, d):
        z = (self.z + d) % 16
        return self.at(zh=z // 4, zl=z % 4)


class Net:
    def __init__(self, send, recv):
        self.send, self.recv, self.started = send, recv, []

    def copy(self, src, dst, device, recv=None):
        n = len(self.started)
        one = pltpu.make_async_remote_copy(
            src_ref=src,
            dst_ref=dst,
            send_sem=self.send.at[n],
            recv_sem=self.recv.at[n] if recv is None else recv,
            device_id=device,
            device_id_type=MESH,
        )
        one.start()
        self.started.append(one)
        return one

    def land(self, ref, recv, device):
        pltpu.make_async_remote_copy(
            src_ref=ref,
            dst_ref=ref,
            send_sem=self.send.at[0],
            recv_sem=recv,
            device_id=device,
            device_id_type=MESH,
        ).wait_recv()

    def drain(self):
        for one in self.started:
            one.wait_send()


def meet(partners):
    barrier = pltpu.get_barrier_semaphore()
    for device in partners:
        pl.semaphore_signal(barrier, inc=1, device_id=device, device_id_type=MESH)
    pl.semaphore_wait(barrier, len(partners))


def rows_of(i, n):
    return pl.ds(pl.multiple_of(i * n, n), n)


def layer_kernel(
    count_hbm, rows_hbm, cols_hbm, features_ref, w_hbm, go_hbm, tiles_ref,
    hid_ref, gx_ref, gw_ref,
    tilebuf, dense, turned, x_ref, acc, part, yland, zsum, zland, w_ref, wt_ref, go_ref, g_ref, dw_ref,
    acc2, back, cland, csum, xland, hsum, hland, w1, w1in, w2in, w4, spots, place_vm, place_ref, count_ref,
    local, send, recv, recv_agg, recv_prop,
):
    me = Place()
    net = Net(send, recv)
    zh, x, core, zl, y = me.zh, me.x, me.core, me.zl, me.y
    sib = me.at(core=1 - core)
    cross = [(e // 4, e % 4) for e in range(1, 16)]

    upper = zl // 2
    inner = zl * (1 - upper) + (3 - zl) * upper
    near = [s * (1 - upper) + (3 - s) * upper for s in (1 - inner, 2, 3)]
    near.append(zl)

    def fetch(src, dst, n):
        one = pltpu.make_async_copy(src, dst, local.at[n])
        one.start()
        return one

    own_in = fetch(features_ref, x_ref.at[zh, x, core], 0)
    count_in = fetch(count_hbm, count_ref, 7)
    rows_in = fetch(rows_hbm, spots.at[0], 4)
    cols_in = fetch(cols_hbm, spots.at[1], 5)
    tiles_in = fetch(tiles_ref, tilebuf.at[pl.ds(0, 128)], 1)
    w_in = fetch(w_hbm, w_ref, 2)
    go_in = fetch(go_hbm, go_ref, 3)
    meet(
        [sib, me.at(zh=zh + 1), me.at(zh=zh - 1)]
        + [me.at(x=x + d) for d in (1, 2, 3)]
        + [me.at(y=y + d) for d in (1, 2, 3)]
        + [me.at(zl=zl + d) for d in (1, 2, 3)]
    )
    own_in.wait()

    def slot(a, b):
        return x_ref.at[a % 4, b % 4, core]

    over_z, over_x, over_c = {}, {}, {}
    for d in (1, 3):
        over_z[d] = net.copy(slot(zh, x), slot(zh, x), me.at(zh=zh + d))

    def pass_on(d, half):
        part_of = slot(zh - d, x).at[pl.ds(half * 64, 64)]
        over_z[d, half] = net.copy(part_of, part_of, me.at(zh=zh + d))

    def send_c(d, e):
        over_c[d, e] = net.copy(slot(zh - d, x - e), slot(zh - d, x - e), sib)

    def send_x(d):
        for e in (2, 1, 3):
            over_x[d, e] = net.copy(slot(zh - d, x), slot(zh - d, x), me.at(x=x + e))
        send_c(d, 0)

    def land_x(d):
        for e in (1, 3, 2):
            over_x[d, e].wait_recv()
            send_c(d, e)

    def land_c(d):
        for e in range(4):
            over_c[d, e].wait_recv()

    send_x(0)

    count_in.wait()
    rows_in.wait()
    cols_in.wait()
    lane = lax.broadcasted_iota(jnp.int32, (T, T), 1)
    slot_id = lax.broadcasted_iota(jnp.int32, (T, T), 0)
    spot = jnp.where(lane < count_ref[0, 0], spots[0] * 32 + spots[1], -1)
    spot = jnp.sum(jnp.where(lane == slot_id, spot, 0), axis=1, keepdims=True)
    hit = spot == lax.broadcasted_iota(jnp.int32, (T, 512), 1)
    found = jnp.where(hit, lax.broadcasted_iota(jnp.int32, (T, 512), 0) - 128, 0)
    place_vm[...] = jnp.sum(found, axis=0, keepdims=True) + 128
    place_in = fetch(place_vm, place_ref, 6)
    tilebuf[128] = jnp.zeros((T, T), BF)
    tiles_in.wait()
    place_in.wait()

    def build(r, _):
        for c in range(32):
            dense[c // 8, rows_of(r, T), pl.ds((c % 8) * T, T)] = tilebuf[place_ref[0, r * 32 + c]]
        return 0

    lax.fori_loop(0, 16, build, 0)
    land_x(0)

    def turn(s, _):
        for j in range(8):
            tilebuf[s * 8 + j] = tilebuf[s * 8 + j].T
        return 0

    def build_back(k):
        def step(c, _):
            for j in range(4):
                turned[k, rows_of(c, T), pl.ds(j * T, T)] = tilebuf[place_ref[0, (k * 4 + j) * 32 + c]]
            return 0

        lax.fori_loop(0, 32, step, 0)

    lax.fori_loop(0, 16, turn, 0)

    def forward(d, first):
        a = (zh - d) % 4
        xs = x_ref.at[a].reshape(1024, F)

        def block(m, _):
            more = jnp.dot(dense[a, rows_of(m, 1024)], xs[...], preferred_element_type=F32)
            if first:
                acc[rows_of(m, 1024)] = more
            else:
                acc[rows_of(m, 1024)] += more
            return 0

        lax.fori_loop(0, 2, block, 0)

    over_z[1].wait_recv()
    pass_on(1, 0)
    send_x(1)
    over_z[3].wait_recv()
    pass_on(3, 1)
    send_x(3)
    land_c(0)
    forward(0, True)
    build_back((zl + 3) % 4)
    land_x(1)
    land_x(3)
    over_z[1, 0].wait_recv()
    over_z[3, 1].wait_recv()
    send_x(2)
    land_c(1)
    forward(1, False)
    land_c(3)
    forward(3, False)
    land_x(2)
    land_c(2)

    far = (zh + 2) % 4
    last_x = x_ref.at[far].reshape(1024, F)
    over_y = {}
    for k in (2, 1, 0, 3):
        q = near[k]
        more = jnp.dot(dense[far, rows_of(q, 512)], last_x[...], preferred_element_type=F32)
        part[q] = (acc[rows_of(q, 512)] + more).astype(BF).reshape(4, T, F)
        for e in (2, 1, 3):
            over_y[k, e] = net.copy(part.at[q, (y + e) % 4], yland.at[k, e - 1], me.at(y=y + e))

    for i, k in enumerate((2, 1, 0, 3)):
        if i:
            build_back((zl + 3 - i) % 4)
        total = part[near[k], y].astype(F32)
        for e in (1, 3, 2):
            over_y[k, e].wait_recv()
            total += yland[k, e - 1].astype(F32)
        if k < 3:
            zsum[k] = total.astype(BF)
            net.copy(zsum.at[k], zland.at[zl], me.at(zl=near[k]), recv_agg.at[zl])

    w_in.wait()
    wt_ref[...] = w_ref[...].T
    go_in.wait()
    for k in range(3):
        net.land(zland.at[near[k]], recv_agg.at[near[k]], me.at(zl=near[k]))
        total += zland[near[k]].astype(F32)
    agg = total.astype(BF)

    w = w_ref[...]
    pre = jnp.dot(agg, w, preferred_element_type=F32)
    erf = lax.erf(pre * root_half)
    slope = 0.5 * (1.0 + erf) + pre * jnp.exp(-0.5 * pre * pre) * inv_root_tau
    pre_grad = (go_ref[...].astype(F32) * slope).astype(BF)
    prop = jnp.dot(pre_grad, wt_ref[...], preferred_element_type=F32)
    g_ref[zl, y] = prop.astype(BF)

    def gslot(a, b):
        return g_ref.at[a % 4, b % 4]

    back_y = {}
    for k in (2, 1, 0):
        net.copy(gslot(zl, y), gslot(zl, y), me.at(zl=near[k]), recv_prop.at[zl])

    def send_y(k):
        for e in (2, 1, 3):
            back_y[k, e] = net.copy(gslot(near[k], y), gslot(near[k], y), me.at(y=y + e))

    def land_y(k):
        for e in (1, 3, 2):
            back_y[k, e].wait_recv()

    send_y(3)
    hid_ref[...] = (0.5 * pre * (1.0 + erf)).astype(BF)
    dw_ref[...] = lax.dot_general(agg, pre_grad, (((0,), (0,)), ((), ())), preferred_element_type=F32)
    w_core = net.copy(dw_ref.at[rows_of(1 - core, T)], w1in, sib)

    w_core.wait_recv()
    w1[...] = dw_ref[rows_of(core, T)] + w1in[...]

    def piece(ref, dx, dy):
        return ref.at[rows_of((x + dx) % 4 * 4 + (y + dy) % 4, 8)]

    w_cross = [
        net.copy(piece(w1, dx, dy), w2in.at[dx * 4 + dy - 1], me.at(x=x + dx, y=y + dy))
        for dx, dy in cross
    ]
    for k in range(3):
        net.land(gslot(near[k], y), recv_prop.at[near[k]], me.at(zl=near[k]))
        send_y(k)

    def backward(k, first):
        a = near[k]
        gs = g_ref.at[a].reshape(512, F)

        def block(m, _):
            more = jnp.dot(turned[a, rows_of(m, 2048)], gs[...], preferred_element_type=F32)
            if first:
                acc2[rows_of(m, 2048)] = more
            else:
                acc2[rows_of(m, 2048)] += more
            return 0

        lax.fori_loop(0, 2, block, 0)

    land_y(3)
    backward(3, True)
    for one in w_cross:
        one.wait_recv()
    total = piece(w1, 0, 0)[...]
    for e in range(15):
        total += w2in[e]
    w4[me.z] = total
    w_z = [net.copy(w4.at[me.z], w4.at[me.z], me.along_z(d)) for d in range(1, 16)]
    for k in range(2):
        land_y(k)
        backward(k, False)
    land_y(2)

    last = near[2]
    last_g = g_ref.at[last].reshape(512, F)
    order = (2, 1, 3, 0)
    swaps, back_x, back_z = {}, {}, {}
    for d in order:
        q = (zh + d) % 4
        more = jnp.dot(turned[last, rows_of(q, 1024)], last_g[...], preferred_element_type=F32)
        back[q] = (acc2[rows_of(q, 1024)] + more).astype(BF).reshape(4, 2, T, F)
        swaps[d] = net.copy(back.at[q, :, 1 - core], cland.at[d], sib)
    for d in order:
        q = (zh + d) % 4
        swaps[d].wait_recv()
        csum[d] = (back[q, :, core].astype(F32) + cland[d].astype(F32)).astype(BF)
        for e in (2, 1, 3):
            back_x[d, e] = net.copy(csum.at[d, (x + e) % 4], xland.at[d, e - 1], me.at(x=x + e))

    def land_back(d):
        total = csum[d, x].astype(F32)
        for e in (1, 3, 2):
            back_x[d, e].wait_recv()
            total += xland[d, e - 1].astype(F32)
        if d:
            hsum[d - 1] = total.astype(BF)
            back_z[d] = net.copy(hsum.at[d - 1], hland.at[d - 1], me.at(zh=zh + d))
        return total

    land_back(2)
    land_back(1)
    land_back(3)
    for one in w_z:
        one.wait_recv()
    mine = gw_ref.at[core, rows_of(x * 4 + y, 8)]
    mine[...] = jnp.sum(w4[...], axis=0)
    w_back = [net.copy(mine, mine, me.at(x=x + dx, y=y + dy)) for dx, dy in cross]
    total = land_back(0)
    for one in w_back:
        one.wait_recv()
    w_last = net.copy(gw_ref.at[core], gw_ref.at[core], sib)
    for d in (1, 3):
        back_z[d].wait_recv()
        total += hland[d - 1].astype(F32)
    back_z[2].wait_recv()
    gx_ref[...] = (total + hland[1].astype(F32)).astype(BF)
    w_last.wait_recv()
    net.drain()


VM = pl.BlockSpec(memory_space=pltpu.VMEM)
ANY = pl.BlockSpec(memory_space=pl.ANY)
DMA = pltpu.SemaphoreType.DMA


def shape(*dims, dtype=BF):
    return jax.ShapeDtypeStruct(dims, dtype)


def hand_over_kernel(a_ref, b_ref, c_ref, a_out, b_out, c_out, a_mid, b_mid, c_mid, sems):
    triples = ((a_ref, a_mid, a_out), (b_ref, b_mid, b_out), (c_ref, c_mid, c_out))
    inward = [pltpu.make_async_copy(src, mid, sems.at[0, n]) for n, (src, mid, _) in enumerate(triples)]
    outward = [pltpu.make_async_copy(mid, dst, sems.at[1, n]) for n, (_, mid, dst) in enumerate(triples)]
    for one in inward:
        one.start()
    for one, other in zip(inward, outward):
        one.wait()
        other.start()
    for one in outward:
        one.wait()


def body(features, weight, grad_out, tiles, tile_rows, tile_cols, tile_count):
    b16 = lambda *dims: pltpu.VMEM(dims, BF)
    b32 = lambda *dims: pltpu.VMEM(dims, F32)
    found = pl.pallas_call(
        layer_kernel,
        out_shape=[shape(T, F), shape(T, F), shape(2, T, F, dtype=F32)],
        in_specs=[ANY] * 7,
        out_specs=[VM] * 3,
        scratch_shapes=[
            b16(129, T, T),
            b16(4, 2048, 1024),
            b16(4, 4096, 512),
            b16(4, 4, 2, T, F),
            b32(2048, F),
            b16(4, 4, T, F),
            b16(4, 3, T, F),
            b16(3, T, F),
            b16(4, T, F),
            b16(F, F),
            b16(F, F),
            b16(T, F),
            b16(4, 4, T, F),
            b32(F, F),
            b32(4096, F),
            b16(4, 4, 2, T, F),
            b16(4, 4, T, F),
            b16(4, 4, T, F),
            b16(4, 3, T, F),
            b16(3, T, F),
            b16(3, T, F),
            b32(T, F),
            b32(T, F),
            b32(15, 8, F),
            b32(16, 8, F),
            pltpu.VMEM((2, 1, T), jnp.int32),
            pltpu.VMEM((1, 512), jnp.int32),
            pltpu.SMEM((1, 512), jnp.int32),
            pltpu.SMEM((1, 1), jnp.int32),
            DMA((8,)),
            DMA((144,)),
            DMA((144,)),
            DMA((4,)),
            DMA((4,)),
        ],
        compiler_params=pltpu.CompilerParams(
            collective_id=0, has_side_effects=True, vmem_limit_bytes=57 * 2**20
        ),
    )(
        tile_count,
        tile_rows.reshape(1, T),
        tile_cols.reshape(1, T),
        features,
        weight,
        grad_out,
        tiles.reshape(128, T, T),
    )
    hidden, grad_features, grad_weight = pl.pallas_call(
        hand_over_kernel,
        out_shape=[shape(T, F), shape(T, F), shape(2, T, F, dtype=F32)],
        in_specs=[ANY] * 3,
        out_specs=[ANY] * 3,
        scratch_shapes=[b16(T, F), b16(T, F), b32(2, T, F), DMA((2, 3))],
    )(*found)
    return hidden, grad_features, grad_weight.reshape(F, F)


def solution(mesh):
    return jax.shard_map(
        body,
        mesh=mesh,
        in_specs=(
            P(("col", "row"), None),
            P(),
            P(("row", "col"), None),
            P("row", "col", None, None, None),
            P("row", "col", None),
            P("row", "col", None),
            P("row", "col"),
        ),
        out_specs=(P(("row", "col"), None), P(("col", "row"), None), P()),
        check_vma=False,
    )
```

```python
import jax
import jax.numpy as jnp
from jax import lax
from jax.experimental import pallas as pl
from jax.experimental.pallas import tpu as pltpu
from jax.sharding import PartitionSpec as P

MESH = pl.DeviceIdType.MESH
BF = jnp.bfloat16
F32 = jnp.float32
root_half = 0.7071067811865476
inv_root_tau = 0.3989422804014327
T = 128
F = 256


class Place:
    def __init__(self):
        row, col = lax.axis_index("row"), lax.axis_index("col")
        self.zh, self.x, self.core = row // 8, (row // 2) % 4, row % 2
        self.zl, self.y = col // 4, col % 4
        self.z = self.zh * 4 + self.zl

    def at(self, zh=None, x=None, core=None, zl=None, y=None):
        zh = self.zh if zh is None else zh % 4
        x = self.x if x is None else x % 4
        core = self.core if core is None else core
        zl = self.zl if zl is None else zl % 4
        y = self.y if y is None else y % 4
        return ((zh * 4 + x) * 2 + core, zl * 4 + y)

    def along_z(self, d):
        z = (self.z + d) % 16
        return self.at(zh=z // 4, zl=z % 4)


class Net:
    def __init__(self, send, recv):
        self.send, self.recv, self.started = send, recv, []

    def copy(self, src, dst, device, recv=None):
        n = len(self.started)
        one = pltpu.make_async_remote_copy(
            src_ref=src,
            dst_ref=dst,
            send_sem=self.send.at[n],
            recv_sem=self.recv.at[n] if recv is None else recv,
            device_id=device,
            device_id_type=MESH,
        )
        one.start()
        self.started.append(one)
        return one

    def land(self, ref, recv, device):
        pltpu.make_async_remote_copy(
            src_ref=ref,
            dst_ref=ref,
            send_sem=self.send.at[0],
            recv_sem=recv,
            device_id=device,
            device_id_type=MESH,
        ).wait_recv()

    def drain(self):
        for one in self.started:
            one.wait_send()


def meet(partners):
    barrier = pltpu.get_barrier_semaphore()
    for device in partners:
        pl.semaphore_signal(barrier, inc=1, device_id=device, device_id_type=MESH)
    pl.semaphore_wait(barrier, len(partners))


def rows_of(i, n):
    return pl.ds(pl.multiple_of(i * n, n), n)


def layer_kernel(
    count_hbm, rows_hbm, cols_hbm, features_ref, w_hbm, go_hbm, tiles_ref,
    hid_ref, gx_ref, gw_ref,
    tilebuf, dense, turned, x_ref, acc, part, yland, zsum, zland, w_ref, wt_ref, go_ref, g_ref, dw_ref,
    acc2, back, cland, csum, xland, hsum, hland, w1, w1in, w2in, w4, spots, place_vm, place_ref, count_ref,
    local, send, recv, recv_agg, recv_prop,
):
    me = Place()
    net = Net(send, recv)
    zh, x, core, zl, y = me.zh, me.x, me.core, me.zl, me.y
    sib = me.at(core=1 - core)
    cross = [(e // 4, e % 4) for e in range(1, 16)]

    upper = zl // 2
    inner = zl * (1 - upper) + (3 - zl) * upper
    near = [s * (1 - upper) + (3 - s) * upper for s in (1 - inner, 2, 3)]
    near.append(zl)

    def fetch(src, dst, n):
        one = pltpu.make_async_copy(src, dst, local.at[n])
        one.start()
        return one

    own_in = fetch(features_ref, x_ref.at[zh, x, core], 0)
    count_in = fetch(count_hbm, count_ref, 7)
    rows_in = fetch(rows_hbm, spots.at[0], 4)
    cols_in = fetch(cols_hbm, spots.at[1], 5)
    tiles_in = fetch(tiles_ref, tilebuf.at[pl.ds(0, 128)], 1)
    w_in = fetch(w_hbm, w_ref, 2)
    go_in = fetch(go_hbm, go_ref, 3)
    meet(
        [sib, me.at(zh=zh + 1), me.at(zh=zh - 1)]
        + [me.at(x=x + d) for d in (1, 2, 3)]
        + [me.at(y=y + d) for d in (1, 2, 3)]
        + [me.at(zl=zl + d) for d in (1, 2, 3)]
    )
    own_in.wait()

    def slot(a, b):
        return x_ref.at[a % 4, b % 4, core]

    over_z, over_x, over_c = {}, {}, {}
    for d in (1, 3):
        over_z[d] = net.copy(slot(zh, x), slot(zh, x), me.at(zh=zh + d))

    def pass_on(d, half):
        part_of = slot(zh - d, x).at[pl.ds(half * 64, 64)]
        over_z[d, half] = net.copy(part_of, part_of, me.at(zh=zh + d))

    def send_c(d, e):
        over_c[d, e] = net.copy(slot(zh - d, x - e), slot(zh - d, x - e), sib)

    def send_x(d):
        for e in (2, 1, 3):
            over_x[d, e] = net.copy(slot(zh - d, x), slot(zh - d, x), me.at(x=x + e))
        send_c(d, 0)

    def land_x(d):
        for e in (1, 3, 2):
            over_x[d, e].wait_recv()
            send_c(d, e)

    def land_c(d):
        for e in range(4):
            over_c[d, e].wait_recv()

    send_x(0)

    count_in.wait()
    rows_in.wait()
    cols_in.wait()
    lane = lax.broadcasted_iota(jnp.int32, (T, T), 1)
    slot_id = lax.broadcasted_iota(jnp.int32, (T, T), 0)
    spot = jnp.where(lane < count_ref[0, 0], spots[0] * 32 + spots[1], -1)
    spot = jnp.sum(jnp.where(lane == slot_id, spot, 0), axis=1, keepdims=True)
    hit = spot == lax.broadcasted_iota(jnp.int32, (T, 512), 1)
    found = jnp.where(hit, lax.broadcasted_iota(jnp.int32, (T, 512), 0) - 128, 0)
    place_vm[...] = jnp.sum(found, axis=0, keepdims=True) + 128
    place_in = fetch(place_vm, place_ref, 6)
    tilebuf[128] = jnp.zeros((T, T), BF)
    tiles_in.wait()
    place_in.wait()

    def build(r, _):
        for c in range(32):
            dense[c // 8, rows_of(r, T), pl.ds((c % 8) * T, T)] = tilebuf[place_ref[0, r * 32 + c]]
        return 0

    lax.fori_loop(0, 16, build, 0)
    land_x(0)

    def turn(s, _):
        for j in range(8):
            tilebuf[s * 8 + j] = tilebuf[s * 8 + j].T
        return 0

    def build_back(k):
        def step(c, _):
            for j in range(4):
                turned[k, rows_of(c, T), pl.ds(j * T, T)] = tilebuf[place_ref[0, (k * 4 + j) * 32 + c]]
            return 0

        lax.fori_loop(0, 32, step, 0)

    lax.fori_loop(0, 16, turn, 0)

    def forward(d, first):
        a = (zh - d) % 4
        xs = x_ref.at[a].reshape(1024, F)

        def block(m, _):
            more = jnp.dot(dense[a, rows_of(m, 1024)], xs[...], preferred_element_type=F32)
            if first:
                acc[rows_of(m, 1024)] = more
            else:
                acc[rows_of(m, 1024)] += more
            return 0

        lax.fori_loop(0, 2, block, 0)

    over_z[1].wait_recv()
    pass_on(1, 0)
    send_x(1)
    over_z[3].wait_recv()
    pass_on(3, 1)
    send_x(3)
    land_c(0)
    forward(0, True)
    build_back((zl + 3) % 4)
    land_x(1)
    land_x(3)
    over_z[1, 0].wait_recv()
    over_z[3, 1].wait_recv()
    send_x(2)
    land_c(1)
    forward(1, False)
    land_c(3)
    forward(3, False)
    land_x(2)
    land_c(2)

    far = (zh + 2) % 4
    last_x = x_ref.at[far].reshape(1024, F)
    over_y = {}
    for k in (2, 1, 0, 3):
        q = near[k]
        more = jnp.dot(dense[far, rows_of(q, 512)], last_x[...], preferred_element_type=F32)
        part[q] = (acc[rows_of(q, 512)] + more).astype(BF).reshape(4, T, F)
        for e in (2, 1, 3):
            over_y[k, e] = net.copy(part.at[q, (y + e) % 4], yland.at[k, e - 1], me.at(y=y + e))

    for i, k in enumerate((2, 1, 0, 3)):
        if i:
            build_back((zl + 3 - i) % 4)
        total = part[near[k], y].astype(F32)
        for e in (1, 3, 2):
            over_y[k, e].wait_recv()
            total += yland[k, e - 1].astype(F32)
        if k < 3:
            zsum[k] = total.astype(BF)
            net.copy(zsum.at[k], zland.at[zl], me.at(zl=near[k]), recv_agg.at[zl])

    w_in.wait()
    wt_ref[...] = w_ref[...].T
    go_in.wait()
    for k in range(3):
        net.land(zland.at[near[k]], recv_agg.at[near[k]], me.at(zl=near[k]))
        total += zland[near[k]].astype(F32)
    agg = total.astype(BF)

    w = w_ref[...]
    pre = jnp.dot(agg, w, preferred_element_type=F32)
    erf = lax.erf(pre * root_half)
    slope = 0.5 * (1.0 + erf) + pre * jnp.exp(-0.5 * pre * pre) * inv_root_tau
    pre_grad = (go_ref[...].astype(F32) * slope).astype(BF)
    prop = jnp.dot(pre_grad, wt_ref[...], preferred_element_type=F32)
    g_ref[zl, y] = prop.astype(BF)

    def gslot(a, b):
        return g_ref.at[a % 4, b % 4]

    back_y = {}
    for k in (2, 1, 0):
        net.copy(gslot(zl, y), gslot(zl, y), me.at(zl=near[k]), recv_prop.at[zl])

    def send_y(k):
        for e in (2, 1, 3):
            back_y[k, e] = net.copy(gslot(near[k], y), gslot(near[k], y), me.at(y=y + e))

    def land_y(k):
        for e in (1, 3, 2):
            back_y[k, e].wait_recv()

    send_y(3)
    dw_ref[...] = lax.dot_general(agg, pre_grad, (((0,), (0,)), ((), ())), preferred_element_type=F32)
    w_core = net.copy(dw_ref.at[rows_of(1 - core, T)], w1in, sib)

    w_core.wait_recv()
    w1[...] = dw_ref[rows_of(core, T)] + w1in[...]

    def piece(ref, dx, dy):
        return ref.at[rows_of((x + dx) % 4 * 4 + (y + dy) % 4, 8)]

    w_cross = [
        net.copy(piece(w1, dx, dy), w2in.at[dx * 4 + dy - 1], me.at(x=x + dx, y=y + dy))
        for dx, dy in cross
    ]
    for k in range(3):
        net.land(gslot(near[k], y), recv_prop.at[near[k]], me.at(zl=near[k]))
        send_y(k)

    def backward(k, first):
        a = near[k]
        gs = g_ref.at[a].reshape(512, F)

        def block(m, _):
            more = jnp.dot(turned[a, rows_of(m, 2048)], gs[...], preferred_element_type=F32)
            if first:
                acc2[rows_of(m, 2048)] = more
            else:
                acc2[rows_of(m, 2048)] += more
            return 0

        lax.fori_loop(0, 2, block, 0)

    hid_ref[...] = (0.5 * pre * (1.0 + erf)).astype(BF)
    land_y(3)
    backward(3, True)
    for one in w_cross:
        one.wait_recv()
    total = piece(w1, 0, 0)[...]
    for e in range(15):
        total += w2in[e]
    w4[me.z] = total
    w_z = [net.copy(w4.at[me.z], w4.at[me.z], me.along_z(d)) for d in range(1, 16)]
    for k in range(2):
        land_y(k)
        backward(k, False)
    land_y(2)

    last = near[2]
    last_g = g_ref.at[last].reshape(512, F)
    order = (2, 1, 3, 0)
    swaps, back_x, back_z = {}, {}, {}
    for d in order:
        q = (zh + d) % 4
        more = jnp.dot(turned[last, rows_of(q, 1024)], last_g[...], preferred_element_type=F32)
        back[q] = (acc2[rows_of(q, 1024)] + more).astype(BF).reshape(4, 2, T, F)
        swaps[d] = net.copy(back.at[q, :, 1 - core], cland.at[d], sib)
    for d in order:
        q = (zh + d) % 4
        swaps[d].wait_recv()
        csum[d] = (back[q, :, core].astype(F32) + cland[d].astype(F32)).astype(BF)
        for e in (2, 1, 3):
            back_x[d, e] = net.copy(csum.at[d, (x + e) % 4], xland.at[d, e - 1], me.at(x=x + e))

    def land_back(d):
        total = csum[d, x].astype(F32)
        for e in (1, 3, 2):
            back_x[d, e].wait_recv()
            total += xland[d, e - 1].astype(F32)
        if d:
            hsum[d - 1] = total.astype(BF)
            back_z[d] = net.copy(hsum.at[d - 1], hland.at[d - 1], me.at(zh=zh + d))
        return total

    land_back(2)
    land_back(1)
    land_back(3)
    for one in w_z:
        one.wait_recv()
    mine = gw_ref.at[core, rows_of(x * 4 + y, 8)]
    mine[...] = jnp.sum(w4[...], axis=0)
    w_back = [net.copy(mine, mine, me.at(x=x + dx, y=y + dy)) for dx, dy in cross]
    total = land_back(0)
    for one in w_back:
        one.wait_recv()
    w_last = net.copy(gw_ref.at[core], gw_ref.at[core], sib)
    for d in (1, 3):
        back_z[d].wait_recv()
        total += hland[d - 1].astype(F32)
    back_z[2].wait_recv()
    gx_ref[...] = (total + hland[1].astype(F32)).astype(BF)
    w_last.wait_recv()
    net.drain()


VM = pl.BlockSpec(memory_space=pltpu.VMEM)
ANY = pl.BlockSpec(memory_space=pl.ANY)
DMA = pltpu.SemaphoreType.DMA


def shape(*dims, dtype=BF):
    return jax.ShapeDtypeStruct(dims, dtype)


def hand_over_kernel(a_ref, b_ref, c_ref, a_out, b_out, c_out, a_mid, b_mid, c_mid, sems):
    triples = ((a_ref, a_mid, a_out), (b_ref, b_mid, b_out), (c_ref, c_mid, c_out))
    inward = [pltpu.make_async_copy(src, mid, sems.at[0, n]) for n, (src, mid, _) in enumerate(triples)]
    outward = [pltpu.make_async_copy(mid, dst, sems.at[1, n]) for n, (_, mid, dst) in enumerate(triples)]
    for one in inward:
        one.start()
    for one, other in zip(inward, outward):
        one.wait()
        other.start()
    for one in outward:
        one.wait()


def body(features, weight, grad_out, tiles, tile_rows, tile_cols, tile_count):
    b16 = lambda *dims: pltpu.VMEM(dims, BF)
    b32 = lambda *dims: pltpu.VMEM(dims, F32)
    found = pl.pallas_call(
        layer_kernel,
        out_shape=[shape(T, F), shape(T, F), shape(2, T, F, dtype=F32)],
        in_specs=[ANY] * 7,
        out_specs=[VM] * 3,
        scratch_shapes=[
            b16(129, T, T),
            b16(4, 2048, 1024),
            b16(4, 4096, 512),
            b16(4, 4, 2, T, F),
            b32(2048, F),
            b16(4, 4, T, F),
            b16(4, 3, T, F),
            b16(3, T, F),
            b16(4, T, F),
            b16(F, F),
            b16(F, F),
            b16(T, F),
            b16(4, 4, T, F),
            b32(F, F),
            b32(4096, F),
            b16(4, 4, 2, T, F),
            b16(4, 4, T, F),
            b16(4, 4, T, F),
            b16(4, 3, T, F),
            b16(3, T, F),
            b16(3, T, F),
            b32(T, F),
            b32(T, F),
            b32(15, 8, F),
            b32(16, 8, F),
            pltpu.VMEM((2, 1, T), jnp.int32),
            pltpu.VMEM((1, 512), jnp.int32),
            pltpu.SMEM((1, 512), jnp.int32),
            pltpu.SMEM((1, 1), jnp.int32),
            DMA((8,)),
            DMA((144,)),
            DMA((144,)),
            DMA((4,)),
            DMA((4,)),
        ],
        compiler_params=pltpu.CompilerParams(
            collective_id=0, has_side_effects=True, vmem_limit_bytes=57 * 2**20
        ),
    )(
        tile_count,
        tile_rows.reshape(1, T),
        tile_cols.reshape(1, T),
        features,
        weight,
        grad_out,
        tiles.reshape(128, T, T),
    )
    hidden, grad_features, grad_weight = pl.pallas_call(
        hand_over_kernel,
        out_shape=[shape(T, F), shape(T, F), shape(2, T, F, dtype=F32)],
        in_specs=[ANY] * 3,
        out_specs=[ANY] * 3,
        scratch_shapes=[b16(T, F), b16(T, F), b32(2, T, F), DMA((2, 3))],
    )(*found)
    return hidden, grad_features, grad_weight.reshape(F, F)


def solution(mesh):
    return jax.shard_map(
        body,
        mesh=mesh,
        in_specs=(
            P(("col", "row"), None),
            P(),
            P(("row", "col"), None),
            P("row", "col", None, None, None),
            P("row", "col", None),
            P("row", "col", None),
            P("row", "col"),
        ),
        out_specs=(P(("row", "col"), None), P(("col", "row"), None), P()),
        check_vma=False,
    )
```
